256 devices in a mesh: dp: 4 (over x), expert: 64 (over z, y, core).
Axes of the slice: x: 4, y: 4, z: 8, core: 2. Of those that a mesh axis runs over, the one named last changes fastest.
Arguments:
- latent: bfloat16 [1024, 1024], P('dp'), may hold values from -6 to 6
- residual: bfloat16 [1024, 4096], P('dp', 'expert'), may hold values from -6 to 6
- gates: float32 [1024, 22], P('dp'), may hold values from 0.1 to 1
- route_ids: int32 [1024, 22], P('dp'), may hold values from 0 to 63, all different within a row; in each aligned block of 256 rows (0 to 255, 256 to 511, ...) at most 184 rows name the same one
- w_gate: bfloat16 [64, 1024, 1344], P('expert', None, 'dp'), may hold values from -0.1875 to 0.1875
- w_up: bfloat16 [64, 1024, 1344], P('expert', None, 'dp'), may hold values from -0.1875 to 0.1875
- w_out: bfloat16 [64, 1344, 1024], P('expert', 'dp'), may hold values from -0.15625 to 0.15625
- w_lift: bfloat16 [1024, 4096], P(None, 'expert'), may hold values from -0.1875 to 0.1875
- norm_gain: bfloat16 [4096], replicated, may hold values from 0.25 to 1.75
- w_vocab: bfloat16 [4096, 65536], P(None, 'expert'), may hold values from -17 to 17
- targets: int32 [1024], P('dp'), may hold values from 0 to 65535
- loss_cot: float32 [1024], P('dp'), may hold values from -64 to 64
Outputs:
- row_loss: float32 [1024], P('dp')
- d_residual: float32 [1024, 4096], P('dp', 'expert')
- d_latent: float32 [1024, 1024], P('dp')
- d_gates: float32 [1024, 22], P('dp')
The draws below stay inside these ranges and needn't reach their ends.
Inputs may be any that keep to these rules, and one draw needn't show every extreme that they name: `route_ids`: each row names 22 different experts. Among the rows of one index of dp no expert is named by more than 184 rows, a bound that some block reaches.
All inputs are finite; a program needn't handle non-finite values.
Results may differ from the reference program's by a relative error of at most 0.04.
Values may be sent and summed in bfloat16 or wider, within the bound.
No kernel may reach another device: no remote copies, remote signals or barrier semaphores. Data moves between devices by JAX's collectives and lax.ppermute only.
A program may use at most 128 MiB of HBM per device.

```python
import math
import jax
import jax.numpy as jnp
import numpy as np
from jax import lax

D = 4096
L = 1024
FF = 1344
TOK_DEV = 256
EXPERTS = 64
TOP = 22
CAP = 184
TOKENS = 1024
VOCAB = 65536
N_DP = 4


def draw_w_vocab(key, part):
    key = jax.random.fold_in(key, 7)
    base = jnp.clip(jax.random.normal(key, (D, VOCAB), jnp.float32), -6.0, 6.0) * (3.0 / math.sqrt(D))
    return base.astype(jnp.bfloat16)


def with_ends(result, rng, low, high):
    longest = result.shape.index(max(result.shape))
    spots = []
    for shift in (0, 1):
        where = [jax.random.randint(jax.random.fold_in(rng, axis), (), 0, length) for axis, length in enumerate(result.shape)]
        where[longest] = (where[longest] + shift) % result.shape[longest]
        spots.append(tuple(where))
    return result.at[spots[0]].set(low).at[spots[1]].set(high)


def levels(key, dims, cuts, smallest, top_value):
    level = 1.0
    for dim, shards_of in cuts:
        draws = jax.random.uniform(jax.random.fold_in(jax.random.fold_in(key, 6), dim), (shards_of,), jnp.float32, smallest / len(cuts), top_value / len(cuts))
        level = level * jnp.repeat(jnp.exp(draws), dims[dim] // shards_of).reshape((-1,) + (1,) * (len(dims) - 1 - dim))
    return level


def assign_block(key, own, number, rows, amount, top, bound, lean):
    order = jax.random.permutation(key, amount)
    packed, common = load_shares(amount, rows * top, bound, lean, True), load_shares(amount, rows * top, bound, lean, False)
    places = jnp.arange(amount)

    def named(tallies, offset_by):
        used = int((tallies > 0).sum())
        fixed = max(1, used // 4)
        moved = fixed + (places - fixed + offset_by * (used - fixed)) % max(1, amount - fixed)
        return jnp.zeros((amount,), jnp.int32).at[order[jnp.where(places < fixed, places, moved)]].set(jnp.asarray(tallies, jnp.int32))

    tallies = jnp.where(number % 4 == 0, named(packed, number // 4), named(common, number - number // 4 - 1))
    mixed = jax.random.permutation(jax.random.fold_in(own, 3), amount)
    source_of, taker = mixed[0:amount // 2 * 2:2], mixed[1:amount // 2 * 2:2]
    room = jnp.minimum(tallies[source_of] - 1, bound - tallies[taker]) // 2
    room = jnp.where((source_of == order[0]) | (taker == order[0]) | (tallies[taker] == 0), 0, jnp.maximum(room, 0))
    moved = jax.random.randint(jax.random.fold_in(own, 4), (amount // 2,), 0, 1 << 20) % (room + 1)
    tallies = tallies.at[source_of].add(-moved).at[taker].add(moved)
    labels = jnp.searchsorted(jnp.cumsum(tallies), jnp.arange(rows * top), side="right").astype(jnp.int32)
    table = labels.reshape(top, rows).T
    table = table[jax.random.permutation(jax.random.fold_in(own, 1), rows)]
    offset_by = jax.random.randint(jax.random.fold_in(own, 2), (rows, 1), 0, top)
    return jnp.take_along_axis(table, (jnp.arange(top)[None, :] + offset_by) % top, axis=1)


def load_shares(number_of, total, most, lean, full):
    portions = [(1 << 20) // math.isqrt(standing ** lean) + 1 for standing in range(1, number_of + 1)]
    largest = most if full else min(most, max(-(-total // number_of), total * portions[0] // sum(portions)))
    least = 1 if total - largest >= number_of - 1 else 0
    counts, rest = [largest] + [least] * (number_of - 1), total - largest - least * (number_of - 1)
    while rest > 0:
        free = [i for i in range(1, number_of) if counts[i] < largest] or [i for i in range(1, number_of) if counts[i] < most]
        pool, remaining = sum([portions[i] for i in free]), rest
        for i in free:
            more = min(most - counts[i], max(1, remaining * portions[i] // pool), rest)
            counts[i] = counts[i] + more
            rest = rest - more
    return np.array(counts)


def bell_draw(rng, shape, width, bound, cuts=(), kind=jnp.bfloat16):
    array = width * jax.random.normal(rng, shape, jnp.float32)
    if cuts:
        array = array * levels(rng, shape, cuts, -0.22, 0.18)
    return jnp.clip(array, -bound, bound).astype(kind)


def setup_inputs(seed: int = 0) -> dict:
    arg_keys = jax.random.split(jax.random.key(seed), 13)
    latent = bell_draw(arg_keys[0], (TOKENS, L), 1.0, 6.0, ((0, 4),))
    residual = bell_draw(arg_keys[1], (TOKENS, D), 1.0, 6.0, ((0, 4), (1, 64)))
    gates = jnp.clip(jnp.exp(math.log(1.0) - 2.3025851 * jax.random.uniform(arg_keys[2], (TOKENS, TOP), jnp.float32) ** levels(arg_keys[2], (TOKENS, TOP), ((0, 4),), -0.2, 0.2)), 0.1, 1.0)
    route_ids_keys = jax.random.split(jax.random.fold_in(arg_keys[3], 1), TOKENS // TOK_DEV)
    route_ids_turns = jax.random.permutation(jax.random.fold_in(arg_keys[3], 3), TOKENS // TOK_DEV)
    route_ids = jax.vmap(lambda own, number: assign_block(jax.random.fold_in(arg_keys[3], 2), own, number, TOK_DEV, EXPERTS, TOP, CAP, 2))(route_ids_keys, route_ids_turns).reshape((TOKENS, TOP))
    w_gate = bell_draw(arg_keys[4], (EXPERTS, L, FF), L ** -0.5, 0.1875, ((0, 64), (2, 4)))
    w_up = bell_draw(arg_keys[5], (EXPERTS, L, FF), L ** -0.5, 0.1875, ((0, 64), (2, 4)))
    w_out = bell_draw(arg_keys[6], (EXPERTS, FF, L), FF ** -0.5, 0.15625, ((0, 64), (1, 4)))
    w_lift = bell_draw(arg_keys[7], (L, D), L ** -0.5, 0.1875, ((1, 64),))
    norm_gain = jnp.clip(1.0 + 0.15 * jax.random.normal(arg_keys[8], (D,), jnp.float32), 0.25, 1.75).astype(jnp.bfloat16)
    w_vocab = draw_w_vocab(jax.random.fold_in(arg_keys[12], 71), 0)
    targets = with_ends(jax.random.randint(arg_keys[10], (TOKENS,), 0, VOCAB), jax.random.fold_in(arg_keys[10], 1), 0, VOCAB - 1).astype(jnp.int32)
    loss_cot = bell_draw(arg_keys[11], (TOKENS,), 16.0, 64.0, ((0, 4),), jnp.float32)
    return dict(latent=latent, residual=residual, gates=gates, route_ids=route_ids, w_gate=w_gate, w_up=w_up, w_out=w_out, w_lift=w_lift, norm_gain=norm_gain, w_vocab=w_vocab, targets=targets, loss_cot=loss_cot)


norm_epsilon = 1e-05

def expert_routing(route_groups, gate_groups, expert_index):
    chosen = route_groups == expert_index
    routed_here = jnp.any(chosen, axis=2)
    gate_own = lax.optimization_barrier(jnp.sum(jnp.where(chosen, gate_groups, 0.0), axis=2))
    slot_index = jnp.cumsum(routed_here.astype(jnp.int32), axis=1) - 1
    slot_range = jnp.arange(CAP, dtype=jnp.int32)
    select = (slot_index[:, None, :] == slot_range[None, :, None]) & routed_here[:, None, :]
    return (chosen, gate_own, select.astype(jnp.float32))

def expert_forward(select, latent_groups, gate_mat, up_mat, out_mat):
    row_block = jnp.einsum('gct,gtl->gcl', select, latent_groups.astype(jnp.float32)).astype(jnp.bfloat16)
    block_float = row_block.astype(jnp.float32)
    gate_pre = jnp.einsum('gcl,lf->gcf', block_float, gate_mat.astype(jnp.float32))
    up_pre = jnp.einsum('gcl,lf->gcf', block_float, up_mat.astype(jnp.float32))
    active = (jax.nn.silu(gate_pre) * up_pre).astype(jnp.bfloat16)
    expert_out = jnp.einsum('gcf,fl->gcl', active.astype(jnp.float32), out_mat.astype(jnp.float32))
    return (gate_pre, up_pre, expert_out)

def reference(latent, residual, gates, route_ids, w_gate, w_up, w_out, w_lift, norm_gain, w_vocab, targets, loss_cot):
    latent_groups = latent.reshape(N_DP, TOK_DEV, L)
    route_groups = route_ids.reshape(N_DP, TOK_DEV, TOP)
    gate_groups = gates.reshape(N_DP, TOK_DEV, TOP)
    expert_ids = jnp.arange(EXPERTS, dtype=jnp.int32)

    def forward_step(carry, expert_index):
        chosen, gate_own, select = expert_routing(route_groups, gate_groups, expert_index)
        gate_pre, up_pre, expert_out = expert_forward(select, latent_groups, w_gate[expert_index], w_up[expert_index], w_out[expert_index])
        routed_out = jnp.einsum('gct,gcl->gtl', select, expert_out)
        return (carry + routed_out * gate_own[..., None], None)
    combined_float, _ = lax.scan(forward_step, jnp.zeros((N_DP, TOK_DEV, L), jnp.float32), expert_ids)
    combined = combined_float.reshape(TOKENS, L).astype(jnp.bfloat16)
    lifted = jnp.dot(combined, w_lift, preferred_element_type=jnp.float32)
    hidden = (residual.astype(jnp.float32) + lifted).astype(jnp.bfloat16)
    hidden_float = hidden.astype(jnp.float32)
    scale_inv = lax.rsqrt(lax.optimization_barrier(jnp.mean(hidden_float * hidden_float, axis=1, keepdims=True)) + norm_epsilon)
    gain_float = norm_gain.astype(jnp.float32)
    normed = (hidden_float * scale_inv * gain_float[None, :]).astype(jnp.bfloat16)
    logits = jnp.dot(normed, w_vocab, preferred_element_type=jnp.float32)
    row_peak = lax.optimization_barrier(jnp.max(logits, axis=1))
    shifted = jnp.exp(logits - row_peak[:, None])
    row_total = lax.optimization_barrier(jnp.sum(shifted, axis=1))
    word_ids = jnp.arange(VOCAB, dtype=jnp.int32)
    is_target = targets[:, None] == word_ids[None, :]
    target_logit = lax.optimization_barrier(jnp.sum(jnp.where(is_target, logits, 0.0), axis=1))
    row_loss = row_peak + jnp.log(row_total) - target_logit
    softmax_probs = shifted / row_total[:, None]
    logit_grad = (loss_cot[:, None] * (softmax_probs - is_target.astype(jnp.float32))).astype(jnp.bfloat16)
    normed_grad = jnp.dot(logit_grad, w_vocab.T, preferred_element_type=jnp.float32)
    scaled = normed_grad * gain_float[None, :]
    inner_term = lax.optimization_barrier(jnp.mean(scaled * hidden_float, axis=1, keepdims=True))
    d_residual = scale_inv * scaled - hidden_float * scale_inv ** 3 * inner_term
    combined_grad = jnp.dot(d_residual.astype(jnp.bfloat16), w_lift.T, preferred_element_type=jnp.float32).astype(jnp.bfloat16)
    comb_groups = combined_grad.astype(jnp.float32).reshape(N_DP, TOK_DEV, L)

    def backward_step(carry, expert_index):
        latent_acc, gate_acc = carry
        chosen, gate_own, select = expert_routing(route_groups, gate_groups, expert_index)
        gate_mat = w_gate[expert_index]
        up_mat = w_up[expert_index]
        out_mat = w_out[expert_index]
        gate_pre, up_pre, expert_out = expert_forward(select, latent_groups, gate_mat, up_mat, out_mat)
        routed_out = jnp.einsum('gct,gcl->gtl', select, expert_out)
        gate_term = lax.optimization_barrier(jnp.sum(comb_groups * routed_out, axis=2))
        gate_acc = gate_acc + jnp.where(chosen, gate_term[..., None], 0.0)
        routed_grad = jnp.einsum('gct,gtl->gcl', select, comb_groups * gate_own[..., None]).astype(jnp.bfloat16)
        act_grad = jnp.einsum('gcl,fl->gcf', routed_grad.astype(jnp.float32), out_mat.astype(jnp.float32))
        sigmoid_gate = jax.nn.sigmoid(gate_pre)
        gate_back = (act_grad * up_pre * sigmoid_gate * (1.0 + gate_pre * (1.0 - sigmoid_gate))).astype(jnp.bfloat16)
        up_back = (act_grad * gate_pre * sigmoid_gate).astype(jnp.bfloat16)
        block_grad = jnp.einsum('gcf,lf->gcl', gate_back.astype(jnp.float32), gate_mat.astype(jnp.float32))
        block_grad = block_grad + jnp.einsum('gcf,lf->gcl', up_back.astype(jnp.float32), up_mat.astype(jnp.float32))
        latent_acc = latent_acc + jnp.einsum('gct,gcl->gtl', select, block_grad)
        return ((latent_acc, gate_acc), None)
    start_carry = (jnp.zeros((N_DP, TOK_DEV, L), jnp.float32), jnp.zeros((N_DP, TOK_DEV, TOP), jnp.float32))
    (latent_acc, gate_acc), _ = lax.scan(backward_step, start_carry, expert_ids)
    return (row_loss, d_residual, latent_acc.reshape(TOKENS, L), gate_acc.reshape(TOKENS, TOP))
```

```python
import jax
import jax.numpy as jnp
from jax import lax
from jax.sharding import Mesh, PartitionSpec as P

norm_epsilon = 1e-05
plane = ("z", "y")
slab = ("z", "y", "c")
bf16 = jnp.bfloat16
f32 = jnp.float32


def dot(a, b, ca, cb):
    return lax.dot_general(a, b, (((ca,), (cb,)), ((), ())), preferred_element_type=f32)


def swap(x):
    return lax.ppermute(x, "c", [(0, 1), (1, 0)])


def deal(x, axes):
    return lax.all_to_all(x, axes, 0, 0, tiled=True)


def spread(x, axes):
    count = lax.axis_size(axes)
    return deal(jnp.broadcast_to(x[None], (count,) + x.shape), axes)


def on_device(
    latent,
    residual,
    gates,
    route_ids,
    w_gate,
    w_up,
    w_out,
    w_lift,
    norm_gain,
    w_vocab,
    targets,
    loss_cot,
):
    core = lax.axis_index("c")
    own_index = lax.axis_index(slab)
    places = lax.axis_size(plane)
    groups = lax.axis_size("dp")
    rows, width = latent.shape
    half = width // 2
    cols = residual.shape[1]
    model = w_vocab.shape[0]
    words = w_vocab.shape[1]
    chunk = rows // places
    first = core == 0

    def mine(x, axis):
        a, b = jnp.split(x, 2, axis)
        return jnp.where(first, a, b)

    def other(x, axis):
        a, b = jnp.split(x, 2, axis)
        return jnp.where(first, b, a)

    def joined(own, peer, axis):
        return jnp.where(
            first,
            jnp.concatenate([own, peer], axis),
            jnp.concatenate([peer, own], axis),
        )

    gate_mat, up_mat, out_mat = w_gate[0], w_up[0], w_out[0]
    chosen = route_ids == own_index
    gate_own = jnp.sum(jnp.where(chosen, gates, 0.0), axis=1)

    gate_groups = [gate_own] + [
        lax.ppermute(gate_own, "dp", [(i, (i + k) % groups) for i in range(groups)])
        for k in range(1, groups)
    ]
    position = lax.axis_index("dp")
    gate_ring = jnp.stack(gate_groups)
    gate_all = jnp.take(gate_ring, (position - jnp.arange(groups)) % groups, axis=0).reshape(-1)
    gate_peer = swap(gate_all)
    out_keep = mine(out_mat, 1)
    out_peer = swap(other(out_mat, 1))

    lat_own = spread(mine(latent, 1), "dp").reshape(groups * rows, half)
    lat_all = joined(lat_own, swap(lat_own), 1)
    gate_pre = dot(lat_all, gate_mat, 1, 0)
    up_pre = dot(lat_all, up_mat, 1, 0)
    active = (jax.nn.silu(gate_pre) * up_pre).astype(bf16)
    active_peer = swap(active)
    part = dot(active, out_keep, 1, 0) * gate_all[:, None]
    part = part + dot(active_peer, out_peer, 1, 0) * gate_peer[:, None]
    summed = jnp.sum(deal(part, "dp").reshape(groups, rows, half), axis=0)
    summed, gate_mat, up_mat, out_mat = lax.optimization_barrier(
        (summed, gate_mat, up_mat, out_mat)
    )
    gate_full = lax.all_gather(gate_mat, "dp")
    up_full = lax.all_gather(up_mat, "dp")
    out_full = lax.all_gather(out_mat, "dp")

    comb_rows = jnp.sum(deal(summed, plane).reshape(places, chunk, half), axis=0).astype(bf16)
    comb_own = spread(comb_rows, plane).reshape(rows, half)
    combined = joined(comb_own, swap(comb_own), 1)
    lifted_t = dot(w_lift, combined, 0, 1)
    hidden_t = (residual.T.astype(f32) + lifted_t).astype(bf16)
    hid_own = spread(hidden_t, plane)
    hid_peer = swap(hid_own)
    hidden_all = joined(hid_own[:, None], hid_peer[:, None], 1).reshape(model, rows)
    hidden_float = hidden_all.astype(f32)
    scale_inv = lax.rsqrt(jnp.mean(hidden_float * hidden_float, axis=0) + norm_epsilon)
    gain_float = norm_gain.astype(f32)
    normed_t = (hidden_float * scale_inv[None, :] * gain_float[:, None]).astype(bf16)
    logits = dot(normed_t, w_vocab, 0, 0)

    word_range = jnp.arange(words, dtype=jnp.int32)
    is_target = targets[:, None] - own_index * words == word_range[None, :]
    target_part = jnp.sum(jnp.where(is_target, logits, 0.0), axis=1)
    peak_part = jnp.max(logits, axis=1)
    below = logits - peak_part[:, None]
    weight = jnp.exp(below)
    total_part = jnp.sum(weight, axis=1)
    lean_part = jnp.sum(weight * below, axis=1)
    stats = jnp.stack([peak_part, total_part, lean_part, target_part]).reshape(-1, 128)
    stats = spread(stats, slab).reshape(-1, 4, rows)
    row_peak = jnp.max(stats[:, 0], axis=0)
    gap = stats[:, 0] - row_peak[None, :]
    share = jnp.exp(gap)
    row_total = jnp.sum(share * stats[:, 1], axis=0)
    lean = jnp.sum(share * (stats[:, 2] + gap * stats[:, 1]), axis=0)
    target_logit = jnp.sum(stats[:, 3], axis=0)
    row_loss = row_peak + jnp.log(row_total) - target_logit
    inner = loss_cot * (lean / row_total - (target_logit - row_peak))

    probs = jnp.exp(logits - row_peak[:, None]) / row_total[:, None]
    logit_grad = (loss_cot[:, None] * (probs - is_target.astype(f32))).astype(bf16)
    grad_t = dot(w_vocab, logit_grad, 1, 1).reshape(places, 2, cols, rows)
    keep_t = jnp.where(first, grad_t[:, 0], grad_t[:, 1])
    send_t = jnp.where(first, grad_t[:, 1], grad_t[:, 0]).astype(bf16)
    keep_t = (keep_t + swap(send_t).astype(f32)).astype(bf16)
    normed_grad = jnp.sum(deal(keep_t, plane).astype(f32), axis=0)
    gain_own = lax.dynamic_slice_in_dim(gain_float, own_index * cols, cols, 0)
    d_res_t = (
        scale_inv[None, :] * (normed_grad * gain_own[:, None])
        - hidden_t.astype(f32) * (scale_inv**2 * (inner / model))[None, :]
    )
    d_residual = d_res_t.T
    d_res_bf = d_res_t.astype(bf16)
    lift_keep = mine(w_lift, 0)
    lift_peer = swap(other(w_lift, 0))
    cg_part = dot(d_res_bf, lift_keep, 0, 1) + dot(swap(d_res_bf), lift_peer, 0, 1)
    cg_rows = deal(cg_part.astype(bf16), plane).astype(f32)
    cg_rows = jnp.sum(cg_rows.reshape(places, chunk, half), axis=0).astype(bf16)
    cg_own = spread(cg_rows, plane).reshape(rows, half)
    comb_grad = joined(cg_own, swap(cg_own), 1)

    gate_pre = jnp.einsum("tl,qlf->qtf", latent, gate_full, preferred_element_type=f32)
    up_pre = jnp.einsum("tl,qlf->qtf", latent, up_full, preferred_element_type=f32)
    sig = jax.nn.sigmoid(gate_pre)
    active = (gate_pre * sig * up_pre).astype(bf16)
    routed_grad = (comb_grad.astype(f32) * gate_own[:, None]).astype(bf16)
    act_grad = jnp.einsum("tl,qfl->qtf", routed_grad, out_full, preferred_element_type=f32)
    gate_term = jnp.sum(act_grad * active.astype(f32), axis=(0, 2))
    gate_term = gate_term / jnp.where(gate_own > 0, gate_own, 1.0)
    gate_back = (act_grad * up_pre * sig * (1.0 + gate_pre * (1.0 - sig))).astype(bf16)
    up_back = (act_grad * gate_pre * sig).astype(bf16)
    block = jnp.einsum("qtf,qlf->tl", gate_back, gate_full, preferred_element_type=f32)
    block = block + jnp.einsum("qtf,qlf->tl", up_back, up_full, preferred_element_type=f32)
    gate_grad = jnp.where(chosen, gate_term[:, None], 0.0)
    gate_grad = jnp.pad(gate_grad, ((0, 0), (0, 128 - gate_grad.shape[1])))
    keep = jnp.concatenate([mine(block, 1), gate_grad], axis=1)
    send = jnp.concatenate([other(block, 1), gate_grad], axis=1).astype(bf16)
    keep = (keep + swap(send).astype(f32)).astype(bf16)
    tail = jnp.sum(deal(keep, plane).astype(f32).reshape(places, chunk, -1), axis=0).astype(bf16)
    tail = spread(tail, plane).reshape(rows, -1)
    d_latent = joined(tail[:, :half], swap(tail[:, :half]), 1).astype(f32)
    d_gates = tail[:, half : half + gates.shape[1]].astype(f32)
    return (row_loss, d_residual, d_latent, d_gates)


def solution(mesh):
    fine = Mesh(mesh.devices.reshape(mesh.devices.shape[0], 8, 4, 2), ("dp", "z", "y", "c"))
    in_specs = (
        P("dp", None),
        P("dp", slab),
        P("dp", None),
        P("dp", None),
        P(slab, None, "dp"),
        P(slab, None, "dp"),
        P(slab, "dp", None),
        P(None, slab),
        P(),
        P(None, slab),
        P("dp"),
        P("dp"),
    )
    out_specs = (P("dp"), P("dp", slab), P("dp", None), P("dp", None))
    return jax.shard_map(
        on_device, mesh=fine, in_specs=in_specs, out_specs=out_specs, check_vma=False
    )
```

```python
import jax
import jax.numpy as jnp
from jax import lax
from jax.sharding import Mesh, PartitionSpec as P

norm_epsilon = 1e-05
plane = ("z", "y")
slab = ("z", "y", "c")
bf16 = jnp.bfloat16
f32 = jnp.float32


def dot(a, b, ca, cb):
    return lax.dot_general(a, b, (((ca,), (cb,)), ((), ())), preferred_element_type=f32)


def swap(x):
    return lax.ppermute(x, "c", [(0, 1), (1, 0)])


def deal(x, axes):
    return lax.all_to_all(x, axes, 0, 0, tiled=True)


def spread(x, axes):
    count = lax.axis_size(axes)
    return deal(jnp.broadcast_to(x[None], (count,) + x.shape), axes)


def on_device(
    latent,
    residual,
    gates,
    route_ids,
    w_gate,
    w_up,
    w_out,
    w_lift,
    norm_gain,
    w_vocab,
    targets,
    loss_cot,
):
    core = lax.axis_index("c")
    own_index = lax.axis_index(slab)
    places = lax.axis_size(plane)
    rows, width = latent.shape
    half = width // 2
    cols = residual.shape[1]
    model = w_vocab.shape[0]
    words = w_vocab.shape[1]
    chunk = rows // places
    first = core == 0

    def mine(x, axis):
        a, b = jnp.split(x, 2, axis)
        return jnp.where(first, a, b)

    def other(x, axis):
        a, b = jnp.split(x, 2, axis)
        return jnp.where(first, b, a)

    def joined(own, peer, axis):
        return jnp.where(
            first,
            jnp.concatenate([own, peer], axis),
            jnp.concatenate([peer, own], axis),
        )

    gate_mat, up_mat, out_mat = w_gate[0], w_up[0], w_out[0]
    chosen = route_ids == own_index
    gate_own = jnp.sum(jnp.where(chosen, gates, 0.0), axis=1)

    out_full = lax.all_gather(out_mat, "dp")

    lat_own = spread(mine(latent, 1), "dp")
    lat_all = joined(lat_own, swap(lat_own), 2)
    gate_part = jnp.einsum("gtl,lf->gtf", lat_all, gate_mat, preferred_element_type=f32)
    up_part = jnp.einsum("gtl,lf->gtf", lat_all, up_mat, preferred_element_type=f32)
    active = (jax.nn.silu(gate_part) * up_part).astype(bf16)
    active = deal(active, "dp")
    active, gate_mat, up_mat = lax.optimization_barrier((active, gate_mat, up_mat))
    gate_full = lax.all_gather(gate_mat, "dp")
    up_full = lax.all_gather(up_mat, "dp")
    part = jnp.einsum("qtf,qfl->tl", active, out_full, preferred_element_type=f32)
    part = part * gate_own[:, None]
    summed = mine(part, 1) + swap(other(part, 1))

    comb_rows = jnp.sum(deal(summed, plane).reshape(places, chunk, half), axis=0).astype(bf16)
    comb_own = spread(comb_rows, plane).reshape(rows, half)
    combined = joined(comb_own, swap(comb_own), 1)
    lifted_t = dot(w_lift, combined, 0, 1)
    hidden_t = (residual.T.astype(f32) + lifted_t).astype(bf16)
    hid_own = spread(hidden_t, plane)
    hid_peer = swap(hid_own)
    hidden_all = joined(hid_own[:, None], hid_peer[:, None], 1).reshape(model, rows)
    hidden_float = hidden_all.astype(f32)
    scale_inv = lax.rsqrt(jnp.mean(hidden_float * hidden_float, axis=0) + norm_epsilon)
    gain_float = norm_gain.astype(f32)
    normed_t = (hidden_float * scale_inv[None, :] * gain_float[:, None]).astype(bf16)
    logits = dot(normed_t, w_vocab, 0, 0)

    word_range = jnp.arange(words, dtype=jnp.int32)
    is_target = targets[:, None] - own_index * words == word_range[None, :]
    target_part = jnp.sum(jnp.where(is_target, logits, 0.0), axis=1)
    peak_part = jnp.max(logits, axis=1)
    below = logits - peak_part[:, None]
    weight = jnp.exp(below)
    total_part = jnp.sum(weight, axis=1)
    lean_part = jnp.sum(weight * below, axis=1)
    stats = jnp.stack([peak_part, total_part, lean_part, target_part]).reshape(-1, 128)
    stats = spread(stats, slab).reshape(-1, 4, rows)
    row_peak = jnp.max(stats[:, 0], axis=0)
    gap = stats[:, 0] - row_peak[None, :]
    share = jnp.exp(gap)
    row_total = jnp.sum(share * stats[:, 1], axis=0)
    lean = jnp.sum(share * (stats[:, 2] + gap * stats[:, 1]), axis=0)
    target_logit = jnp.sum(stats[:, 3], axis=0)
    row_loss = row_peak + jnp.log(row_total) - target_logit
    inner = loss_cot * (lean / row_total - (target_logit - row_peak))

    probs = jnp.exp(logits - row_peak[:, None]) / row_total[:, None]
    logit_grad = (loss_cot[:, None] * (probs - is_target.astype(f32))).astype(bf16)
    grad_t = dot(w_vocab, logit_grad, 1, 1).reshape(places, 2, cols, rows)
    keep_t = jnp.where(first, grad_t[:, 0], grad_t[:, 1])
    send_t = jnp.where(first, grad_t[:, 1], grad_t[:, 0]).astype(bf16)
    keep_t = (keep_t + swap(send_t).astype(f32)).astype(bf16)
    normed_grad = jnp.sum(deal(keep_t, plane).astype(f32), axis=0)
    gain_own = lax.dynamic_slice_in_dim(gain_float, own_index * cols, cols, 0)
    d_res_t = (
        scale_inv[None, :] * (normed_grad * gain_own[:, None])
        - hidden_t.astype(f32) * (scale_inv**2 * (inner / model))[None, :]
    )
    d_residual = d_res_t.T
    d_res_bf = d_res_t.astype(bf16)
    lift_keep = mine(w_lift, 0)
    lift_peer = swap(other(w_lift, 0))
    cg_part = dot(d_res_bf, lift_keep, 0, 1) + dot(swap(d_res_bf), lift_peer, 0, 1)
    cg_rows = deal(cg_part.astype(bf16), plane).astype(f32)
    cg_rows = jnp.sum(cg_rows.reshape(places, chunk, half), axis=0).astype(bf16)
    cg_own = spread(cg_rows, plane).reshape(rows, half)
    comb_grad = joined(cg_own, swap(cg_own), 1)

    gate_pre = jnp.einsum("tl,qlf->qtf", latent, gate_full, preferred_element_type=f32)
    up_pre = jnp.einsum("tl,qlf->qtf", latent, up_full, preferred_element_type=f32)
    sig = jax.nn.sigmoid(gate_pre)
    routed_grad = (comb_grad.astype(f32) * gate_own[:, None]).astype(bf16)
    act_grad = jnp.einsum("tl,qfl->qtf", routed_grad, out_full, preferred_element_type=f32)
    gate_term = jnp.sum(act_grad * active.astype(f32), axis=(0, 2))
    gate_term = gate_term / jnp.where(gate_own > 0, gate_own, 1.0)
    gate_back = (act_grad * up_pre * sig * (1.0 + gate_pre * (1.0 - sig))).astype(bf16)
    up_back = (act_grad * gate_pre * sig).astype(bf16)
    block = jnp.einsum("qtf,qlf->tl", gate_back, gate_full, preferred_element_type=f32)
    block = block + jnp.einsum("qtf,qlf->tl", up_back, up_full, preferred_element_type=f32)
    gate_grad = jnp.where(chosen, gate_term[:, None], 0.0)
    gate_grad = jnp.pad(gate_grad, ((0, 0), (0, 128 - gate_grad.shape[1])))
    keep = jnp.concatenate([mine(block, 1), gate_grad], axis=1)
    send = jnp.concatenate([other(block, 1), gate_grad], axis=1).astype(bf16)
    keep = (keep + swap(send).astype(f32)).astype(bf16)
    tail = jnp.sum(deal(keep, plane).astype(f32).reshape(places, chunk, -1), axis=0).astype(bf16)
    tail = spread(tail, plane).reshape(rows, -1)
    d_latent = joined(tail[:, :half], swap(tail[:, :half]), 1).astype(f32)
    d_gates = tail[:, half : half + gates.shape[1]].astype(f32)
    return (row_loss, d_residual, d_latent, d_gates)


def solution(mesh):
    fine = Mesh(mesh.devices.reshape(mesh.devices.shape[0], 8, 4, 2), ("dp", "z", "y", "c"))
    in_specs = (
        P("dp", None),
        P("dp", slab),
        P("dp", None),
        P("dp", None),
        P(slab, None, "dp"),
        P(slab, None, "dp"),
        P(slab, "dp", None),
        P(None, slab),
        P(),
        P(None, slab),
        P("dp"),
        P("dp"),
    )
    out_specs = (P("dp"), P("dp", slab), P("dp", None), P("dp", None))
    return jax.shard_map(
        on_device, mesh=fine, in_specs=in_specs, out_specs=out_specs, check_vma=False
    )
```

```python
import jax
import jax.numpy as jnp
from jax import lax
from jax.experimental import pallas as pl
from jax.experimental.pallas import tpu as pltpu
from jax.sharding import Mesh, PartitionSpec as P

norm_epsilon = 1e-05
plane = ("z", "y")
slab = ("z", "y", "c")
bf16 = jnp.bfloat16
f32 = jnp.float32


def dot(a, b, ca, cb):
    return lax.dot_general(a, b, (((ca,), (cb,)), ((), ())), preferred_element_type=f32)


def swap(x):
    return lax.ppermute(x, "c", [(0, 1), (1, 0)])


def deal(x, axes):
    return lax.all_to_all(x, axes, 0, 0, tiled=True)


def spread(x, axes):
    count = lax.axis_size(axes)
    return deal(jnp.broadcast_to(x[None], (count,) + x.shape), axes)


def compiler_params():
    return pltpu.CompilerParams(vmem_limit_bytes=44 << 20)


def head_kernel(core, own, peer, gain, words, target, logits, stats, block, scale):
    step = pl.program_id(0)
    last = pl.num_programs(0) - 1
    per = gain.shape[2]
    cols = gain.shape[1]
    half = own.shape[0] // per

    @pl.when(step == 0)
    def _():
        def add(i, total):
            a = own[i].astype(f32)
            b = peer[i].astype(f32)
            return total + a * a + b * b

        total = lax.fori_loop(0, own.shape[0], add, jnp.zeros(own.shape[1:], f32), unroll=4)
        mean = jnp.sum(total, axis=0, keepdims=True) / (2 * own.shape[0] * cols) + norm_epsilon
        guess = lax.rsqrt(mean)
        scale[...] = guess * (1.5 - 0.5 * mean * guess * guess)
        logits[...] = jnp.zeros_like(logits)

    def fill(source, base):
        for j in range(per):
            h = source[base + j].astype(f32) * scale[...]
            h = h * gain[0, :, j : j + 1]
            block[j * cols : (j + 1) * cols, :] = h.astype(bf16)

    @pl.when(step < half)
    def _():
        fill(own, step * per)

    @pl.when(step >= half)
    def _():
        fill(peer, (step - half) * per)

    rhs = words[...].reshape(per * cols, -1)
    logits[...] += lax.dot_general(
        block[...], rhs, (((0,), (0,)), ((), ())), preferred_element_type=f32
    )

    @pl.when(step == last)
    def _():
        values = logits[...]
        peak = jnp.max(values, axis=1, keepdims=True)
        below = values - peak
        weight = jnp.exp(below)
        total = jnp.sum(weight, axis=1, keepdims=True)
        lean = jnp.sum(weight * below, axis=1, keepdims=True)
        at = lax.broadcasted_iota(jnp.int32, values.shape, 1) == target[...]
        hit = jnp.sum(jnp.where(at, values, 0.0), axis=1, keepdims=True)
        lane = lax.broadcasted_iota(jnp.int32, (values.shape[0], 128), 1)
        packed = jnp.where(lane == 0, peak, jnp.where(lane == 1, total, 0.0))
        packed = jnp.where(lane == 2, lean, jnp.where(lane == 3, hit, packed))
        row = lax.broadcasted_iota(jnp.int32, stats.shape, 0)
        stats[...] = jnp.where(row == 4, scale[...], packed.T[: stats.shape[0]])


def loss_kernel(core, stats, logits, target, cot, words, grad, send, rows):
    @pl.when(pl.program_id(0) == 0)
    def _():
        peaks = stats[:, 0, :]
        peak = jnp.max(peaks, axis=0, keepdims=True)
        gap = peaks - peak
        share = jnp.exp(gap)
        totals = stats[:, 1, :]
        total = jnp.sum(share * totals, axis=0, keepdims=True)
        lean = jnp.sum(share * (stats[:, 2, :] + gap * totals), axis=0, keepdims=True)
        hit = jnp.sum(stats[:, 3, :], axis=0, keepdims=True)
        inverse = 1.0 / total
        inner = cot[...] * (lean * inverse - (hit - peak))
        row = lax.broadcasted_iota(jnp.int32, (128, peak.shape[1]), 0)
        packed = jnp.where(row == 0, peak, jnp.where(row == 1, inverse, 0.0))
        packed = jnp.where(row == 2, cot[...], packed)
        col = packed.T
        top = lax.broadcasted_iota(jnp.int32, rows.shape, 0)
        loss = peak + jnp.log(total) - hit
        rows[...] = jnp.where(top == 0, loss, jnp.where(top == 1, inner, 0.0))
        probs = jnp.exp(logits[...] - col[:, 0:1]) * col[:, 1:2]
        at = lax.broadcasted_iota(jnp.int32, probs.shape, 1) == target[...]
        grad[...] = (col[:, 2:3] * (probs - jnp.where(at, 1.0, 0.0))).astype(bf16)

    lhs = words[...].reshape(-1, words.shape[3])
    out = lax.dot_general(lhs, grad[...], (((1,), (1,)), ((), ())), preferred_element_type=f32)
    send[...] = out.reshape(send.shape).astype(send.dtype)


def keep_kernel(core, grad, words, keep):
    lhs = words[...].reshape(-1, words.shape[3])
    out = lax.dot_general(lhs, grad[...], (((1,), (1,)), ((), ())), preferred_element_type=f32)
    keep[...] = out.reshape(keep.shape)


def whole(shape):
    return pl.BlockSpec(shape, lambda i, core: (0,) * len(shape))


def call_head(core, own, peer, gain, words, target):
    rows, count = own.shape[2], words.shape[3]
    steps, cols, per = gain.shape
    half = steps // 2

    def part(i, core):
        return (i % half, jnp.where(i < half, core[0], 1 - core[0]), 0, 0)

    return pl.pallas_call(
        head_kernel,
        grid_spec=pltpu.PrefetchScalarGridSpec(
            num_scalar_prefetch=1,
            grid=(steps,),
            in_specs=[
                whole(own.shape),
                whole(peer.shape),
                pl.BlockSpec((1, cols, per), lambda i, core: (i, 0, 0)),
                pl.BlockSpec((per, 1, cols, count), part),
                whole(target.shape),
            ],
            out_specs=[whole((rows, count)), whole((8, rows))],
            scratch_shapes=[
                pltpu.VMEM((per * cols, rows), bf16),
                pltpu.VMEM((1, rows), f32),
            ],
        ),
        out_shape=[
            jax.ShapeDtypeStruct((rows, count), f32),
            jax.ShapeDtypeStruct((8, rows), f32),
        ],
        compiler_params=compiler_params(),
        name="head",
    )(core, own, peer, gain, words, target)


def call_loss(core, stats, logits, target, cot, words, per):
    places, _, cols, count = words.shape
    rows = logits.shape[0]
    return pl.pallas_call(
        loss_kernel,
        grid_spec=pltpu.PrefetchScalarGridSpec(
            num_scalar_prefetch=1,
            grid=(places // per,),
            in_specs=[
                whole(stats.shape),
                whole(logits.shape),
                whole(target.shape),
                whole(cot.shape),
                pl.BlockSpec((per, 1, cols, count), lambda i, core: (i, 1 - core[0], 0, 0)),
            ],
            out_specs=[
                whole((rows, count)),
                pl.BlockSpec((per, cols, rows), lambda i, core: (i, 0, 0)),
                whole((8, rows)),
            ],
        ),
        out_shape=[
            jax.ShapeDtypeStruct((rows, count), bf16),
            jax.ShapeDtypeStruct((places, cols, rows), bf16),
            jax.ShapeDtypeStruct((8, rows), f32),
        ],
        compiler_params=compiler_params(),
        name="loss",
    )(core, stats, logits, target, cot, words)


def call_keep(core, grad, words, per):
    places, _, cols, count = words.shape
    rows = grad.shape[0]
    return pl.pallas_call(
        keep_kernel,
        grid_spec=pltpu.PrefetchScalarGridSpec(
            num_scalar_prefetch=1,
            grid=(places // per,),
            in_specs=[
                whole(grad.shape),
                pl.BlockSpec((per, 1, cols, count), lambda i, core: (i, core[0], 0, 0)),
            ],
            out_specs=pl.BlockSpec((per, cols, rows), lambda i, core: (i, 0, 0)),
        ),
        out_shape=jax.ShapeDtypeStruct((places, cols, rows), f32),
        compiler_params=compiler_params(),
        cost_estimate=pl.CostEstimate(
            flops=places * cols * rows * count * 2,
            bytes_accessed=places * cols * count * 2,
            transcendentals=0,
        ),
        name="keep",
    )(core, grad, words)


def expert_kernel(
    core, own, peer, latent, active, marks, gate_w, up_w, out_w, keep, send, routed, block, term
):
    step = pl.program_id(0)
    half = own.shape[1]
    gate = jnp.sum(marks[...], axis=1, keepdims=True)

    @pl.when(step == 0)
    def _():
        a = (own[...].astype(f32) * gate).astype(bf16)
        b = (peer[...].astype(f32) * gate).astype(bf16)

        @pl.when(core[0] == 0)
        def _():
            routed[:, :half] = a
            routed[:, half:] = b

        @pl.when(core[0] != 0)
        def _():
            routed[:, :half] = b
            routed[:, half:] = a

        block[...] = jnp.zeros_like(block)
        term[...] = jnp.zeros_like(term)

    def over_last(x, w):
        return lax.dot_general(x, w, (((1,), (1,)), ((), ())), preferred_element_type=f32)

    gate_pre = over_last(latent[...], gate_w[0])
    up_pre = over_last(latent[...], up_w[0])
    act_grad = over_last(routed[...], out_w[0])
    sig = 1.0 / (1.0 + jnp.exp(-gate_pre))
    term[...] += jnp.sum(act_grad * active[0].astype(f32), axis=1, keepdims=True)
    gate_back = (act_grad * up_pre * sig * (1.0 + gate_pre * (1.0 - sig))).astype(bf16)
    up_back = (act_grad * gate_pre * sig).astype(bf16)
    block[...] += jnp.dot(gate_back, gate_w[0], preferred_element_type=f32) + jnp.dot(
        up_back, up_w[0], preferred_element_type=f32
    )

    @pl.when(step == pl.num_programs(0) - 1)
    def _():
        share = term[...] / jnp.where(gate > 0, gate, 1.0)
        gate_grad = jnp.where(marks[...] > 0, share, 0.0)
        keep[:, half:] = gate_grad
        send[:, half:] = gate_grad.astype(bf16)

        @pl.when(core[0] == 0)
        def _():
            keep[:, :half] = block[:, :half]
            send[:, :half] = block[:, half:].astype(bf16)

        @pl.when(core[0] != 0)
        def _():
            keep[:, :half] = block[:, half:]
            send[:, :half] = block[:, :half].astype(bf16)


def call_expert(core, own, peer, latent, active, marks, gate_w, up_w, out_w):
    rows, width = latent.shape
    quarters, units, _ = gate_w.shape
    lanes = own.shape[1] + marks.shape[1]

    def part(shape):
        return pl.BlockSpec((1,) + shape, lambda i, core: (i, 0, 0))

    return pl.pallas_call(
        expert_kernel,
        grid_spec=pltpu.PrefetchScalarGridSpec(
            num_scalar_prefetch=1,
            grid=(quarters,),
            in_specs=[
                whole(own.shape),
                whole(peer.shape),
                whole(latent.shape),
                part((rows, units)),
                whole(marks.shape),
                part((units, width)),
                part((units, width)),
                part((units, width)),
            ],
            out_specs=[whole((rows, lanes)), whole((rows, lanes))],
            scratch_shapes=[
                pltpu.VMEM((rows, width), bf16),
                pltpu.VMEM((rows, width), f32),
                pltpu.VMEM((rows, 1), f32),
            ],
        ),
        out_shape=[
            jax.ShapeDtypeStruct((rows, lanes), f32),
            jax.ShapeDtypeStruct((rows, lanes), bf16),
        ],
        compiler_params=compiler_params(),
        name="expert",
    )(core, own, peer, latent, active, marks, gate_w, up_w, out_w)


def on_device(
    latent,
    residual,
    gates,
    route_ids,
    w_gate,
    w_up,
    w_out,
    w_lift,
    norm_gain,
    w_vocab,
    targets,
    loss_cot,
):
    core = lax.axis_index("c")
    own_index = lax.axis_index(slab)
    places = lax.axis_size(plane)
    rows, width = latent.shape
    half = width // 2
    cols = residual.shape[1]
    model = w_vocab.shape[0]
    words = w_vocab.shape[1]
    chunk = rows // places
    first = core == 0

    def mine(x, axis):
        a, b = jnp.split(x, 2, axis)
        return jnp.where(first, a, b)

    def other(x, axis):
        a, b = jnp.split(x, 2, axis)
        return jnp.where(first, b, a)

    def joined(own, peer, axis):
        return jnp.where(
            first,
            jnp.concatenate([own, peer], axis),
            jnp.concatenate([peer, own], axis),
        )

    gate_mat, up_mat, out_mat = w_gate[0], w_up[0], w_out[0]
    chosen = route_ids == own_index
    gate_own = jnp.sum(jnp.where(chosen, gates, 0.0), axis=1)

    out_full = lax.all_gather(out_mat, "dp")

    lat_own = spread(mine(latent, 1), "dp")
    lat_all = joined(lat_own, swap(lat_own), 2)
    gate_part = jnp.einsum("gtl,lf->gtf", lat_all, gate_mat, preferred_element_type=f32)
    up_part = jnp.einsum("gtl,lf->gtf", lat_all, up_mat, preferred_element_type=f32)
    active = (jax.nn.silu(gate_part) * up_part).astype(bf16)
    active = deal(active, "dp")
    active, gate_mat, up_mat = lax.optimization_barrier((active, gate_mat, up_mat))
    gate_full = lax.all_gather(gate_mat.T, "dp")
    up_full = lax.all_gather(up_mat.T, "dp")
    part = jnp.einsum("qtf,qfl->tl", active, out_full, preferred_element_type=f32)
    part = part * gate_own[:, None]
    summed = mine(part, 1) + swap(other(part, 1))

    comb_rows = jnp.sum(deal(summed, plane).reshape(places, chunk, half), axis=0).astype(bf16)
    comb_own = spread(comb_rows, plane).reshape(rows, half)
    combined = joined(comb_own, swap(comb_own), 1)
    lifted_t = dot(w_lift, combined, 0, 1)
    hidden_t = (residual.T.astype(f32) + lifted_t).astype(bf16)
    hid_own = spread(hidden_t, plane)
    hid_peer = swap(hid_own)
    per = 8
    steps = places // per
    core_id = core.astype(jnp.int32)[None]
    gain_float = norm_gain.astype(f32)
    gain_parts = gain_float.reshape(steps, per, 2, cols)
    gain_parts = jnp.concatenate(
        [
            jnp.where(first, gain_parts[:, :, 0], gain_parts[:, :, 1]),
            jnp.where(first, gain_parts[:, :, 1], gain_parts[:, :, 0]),
        ]
    ).transpose(0, 2, 1)
    target = (targets - own_index * words)[:, None]
    vocab = w_vocab.reshape(places, 2, cols, words)
    logits, stats = call_head(core_id, hid_own, hid_peer, gain_parts, vocab, target)
    scale_inv = stats[4]
    stats_all = spread(stats, slab)
    grad, send_t, row_out = call_loss(
        core_id, stats_all, logits, target, loss_cot[None], vocab, per
    )
    row_loss = row_out[0]
    inner = row_out[1]
    keep_t = call_keep(core_id, grad, vocab, per)
    keep_t = (keep_t + swap(send_t).astype(f32)).astype(bf16)
    normed_grad = jnp.sum(deal(keep_t, plane).astype(f32), axis=0)
    gain_own = lax.dynamic_slice_in_dim(gain_float, own_index * cols, cols, 0)
    d_res_t = (
        scale_inv[None, :] * (normed_grad * gain_own[:, None])
        - hidden_t.astype(f32) * (scale_inv**2 * (inner / model))[None, :]
    )
    d_residual = d_res_t.T
    d_res_bf = d_res_t.astype(bf16)
    lift_keep = mine(w_lift, 0)
    lift_peer = swap(other(w_lift, 0))
    cg_part = dot(d_res_bf, lift_keep, 0, 1) + dot(swap(d_res_bf), lift_peer, 0, 1)
    cg_rows = deal(cg_part.astype(bf16), plane).astype(f32)
    cg_rows = jnp.sum(cg_rows.reshape(places, chunk, half), axis=0).astype(bf16)
    cg_own = spread(cg_rows, plane).reshape(rows, half)
    marks = jnp.where(chosen, gates, 0.0)
    marks = jnp.pad(marks, ((0, 0), (0, 128 - marks.shape[1])))
    keep, send = call_expert(
        core_id, cg_own, swap(cg_own), latent, active, marks, gate_full, up_full, out_full
    )
    keep = (keep + swap(send).astype(f32)).astype(bf16)
    tail = jnp.sum(deal(keep, plane).astype(f32).reshape(places, chunk, -1), axis=0).astype(bf16)
    tail = spread(tail, plane).reshape(rows, -1)
    d_latent = joined(tail[:, :half], swap(tail[:, :half]), 1).astype(f32)
    d_gates = tail[:, half : half + gates.shape[1]].astype(f32)
    return (row_loss, d_residual, d_latent, d_gates)


def solution(mesh):
    fine = Mesh(mesh.devices.reshape(mesh.devices.shape[0], 8, 4, 2), ("dp", "z", "y", "c"))
    in_specs = (
        P("dp", None),
        P("dp", slab),
        P("dp", None),
        P("dp", None),
        P(slab, None, "dp"),
        P(slab, None, "dp"),
        P(slab, "dp", None),
        P(None, slab),
        P(),
        P(None, slab),
        P("dp"),
        P("dp"),
    )
    out_specs = (P("dp"), P("dp", slab), P("dp", None), P("dp", None))
    return jax.shard_map(
        on_device, mesh=fine, in_specs=in_specs, out_specs=out_specs, check_vma=False
    )
```

```python
import jax
import jax.numpy as jnp
from jax import lax
from jax.experimental import pallas as pl
from jax.experimental.pallas import tpu as pltpu
from jax.sharding import Mesh, PartitionSpec as P

norm_epsilon = 1e-05
plane = ("z", "y")
slab = ("z", "y", "c")
bf16 = jnp.bfloat16
f32 = jnp.float32


def dot(a, b, ca, cb):
    return lax.dot_general(a, b, (((ca,), (cb,)), ((), ())), preferred_element_type=f32)


def swap(x):
    return lax.ppermute(x, "c", [(0, 1), (1, 0)])


def deal(x, axes):
    return lax.all_to_all(x, axes, 0, 0, tiled=True)


def spread(x, axes):
    count = lax.axis_size(axes)
    return deal(jnp.broadcast_to(x[None], (count,) + x.shape), axes)


def limit(mib):
    return pltpu.CompilerParams(vmem_limit_bytes=mib << 20)


def over_last(x, w):
    return lax.dot_general(x, w, (((1,), (1,)), ((), ())), preferred_element_type=f32)


def head_kernel(core, own, peer, gain, words, target, logits, stats, scale):
    step = pl.program_id(0)
    last = pl.num_programs(0) - 1
    rows, wide = own.shape
    span = gain.shape[2]
    half = wide // span

    @pl.when(step == 0)
    def _():
        total = jnp.zeros((rows, 128), f32)
        for k in range(wide // 128):
            a = own[:, k * 128 : (k + 1) * 128].astype(f32)
            b = peer[:, k * 128 : (k + 1) * 128].astype(f32)
            total = total + a * a + b * b
        mean = jnp.sum(total, axis=1, keepdims=True) / (2 * wide) + norm_epsilon
        guess = lax.rsqrt(mean)
        guess = guess * (1.5 - 0.5 * mean * guess * guess)
        scale[...] = jnp.broadcast_to(guess, scale.shape)

    def add(source, index):
        h = source[:, pl.ds(pl.multiple_of(index * span, span), span)].astype(f32)
        h = (h * scale[:, 0:1] * gain[0]).astype(bf16)
        rhs = words[...].reshape(span, -1)
        part = jnp.dot(h, rhs, preferred_element_type=f32)

        @pl.when(step == 0)
        def _():
            logits[...] = part

        @pl.when(step > 0)
        def _():
            logits[...] += part

    @pl.when(step < half)
    def _():
        add(own, step)

    @pl.when(step >= half)
    def _():
        add(peer, step - half)

    @pl.when(step == last)
    def _():
        values = logits[...]
        peak = jnp.max(values, axis=1, keepdims=True)
        below = values - peak
        weight = jnp.exp(below)
        total = jnp.sum(weight, axis=1, keepdims=True)
        lean = jnp.sum(weight * below, axis=1, keepdims=True)
        at = lax.broadcasted_iota(jnp.int32, values.shape, 1) == target[...]
        hit = jnp.sum(jnp.where(at, values, 0.0), axis=1, keepdims=True)
        lane = lax.broadcasted_iota(jnp.int32, (rows, 128), 1)
        packed = jnp.where(lane == 0, peak, jnp.where(lane == 1, total, 0.0))
        packed = jnp.where(lane == 2, lean, jnp.where(lane == 3, hit, packed))
        packed = packed.T
        stats[0:4, :] = packed[0:4, 0:128]
        stats[4:8, :] = packed[0:4, 128:256]


def loss_kernel(core, stats, logits, target, cot, scale, words, grad, send, loss, marks):
    @pl.when(pl.program_id(0) == 0)
    def _():
        def stat(k):
            return jnp.concatenate([stats[:, k, :], stats[:, k + 4, :]], axis=1)

        peaks = stat(0)
        peak = jnp.max(peaks, axis=0, keepdims=True)
        gap = peaks - peak
        share = jnp.exp(gap)
        totals = stat(1)
        total = jnp.sum(share * totals, axis=0, keepdims=True)
        lean = jnp.sum(share * (stat(2) + gap * totals), axis=0, keepdims=True)
        hit = jnp.sum(stat(3), axis=0, keepdims=True)
        inverse = 1.0 / total
        inner = cot[...] * (lean * inverse - (hit - peak))
        row = lax.broadcasted_iota(jnp.int32, (128, peak.shape[1]), 0)
        packed = jnp.where(row == 0, peak, jnp.where(row == 1, inverse, 0.0))
        packed = jnp.where(row == 2, cot[...], jnp.where(row == 3, inner, packed))
        col = packed.T
        loss[...] = jnp.broadcast_to(peak + jnp.log(total) - hit, loss.shape)
        lane = lax.broadcasted_iota(jnp.int32, marks.shape, 1)
        marks[...] = jnp.where(lane == 0, scale[...], col[:, 3:4])
        probs = jnp.exp(logits[...] - col[:, 0:1]) * col[:, 1:2]
        at = lax.broadcasted_iota(jnp.int32, probs.shape, 1) == target[...]
        grad[...] = (col[:, 2:3] * (probs - jnp.where(at, 1.0, 0.0))).astype(bf16)

    rhs = words[...].reshape(-1, words.shape[3])
    send[...] = over_last(grad[...], rhs).astype(send.dtype)


def keep_kernel(core, grad, words, keep):
    keep[...] = over_last(grad[...], words[...].reshape(-1, words.shape[3]))


def lower_kernel(place, parts, hidden, gain, marks, lift, chunks, partial):
    total = jnp.sum(parts[...].astype(f32), axis=0)
    scale = marks[:, 0:1]
    inner = marks[:, 1:2]
    model = 2 * hidden.shape[1]
    d_res = scale * (total * gain[...])
    d_res = d_res - hidden[...].astype(f32) * (scale * scale * (inner / model))
    high = d_res.astype(bf16)
    low = (d_res - high.astype(f32)).astype(bf16)
    cols = chunks.shape[2] // 2
    for k in range(chunks.shape[0]):
        chunks[k, :, :cols] = high[:, k * cols : (k + 1) * cols]
        chunks[k, :, cols:] = low[:, k * cols : (k + 1) * cols]
    partial[...] = jnp.dot(high, lift[...], preferred_element_type=f32)


def expert_kernel(
    core, own, peer, latent, marks, gate_w, up_w, out_w, keep, send, routed, block, term
):
    step = pl.program_id(0)
    half = own.shape[1]
    width = latent.shape[1]
    gate = jnp.sum(marks[...], axis=1, keepdims=True)

    @pl.when(step == 0)
    def _():
        a = (own[...].astype(f32) * gate).astype(bf16)
        b = (peer[...].astype(f32) * gate).astype(bf16)

        @pl.when(core[0] == 0)
        def _():
            routed[:, :half] = a
            routed[:, half:] = b

        @pl.when(core[0] != 0)
        def _():
            routed[:, :half] = b
            routed[:, half:] = a

        block[...] = jnp.zeros_like(block)
        term[...] = jnp.zeros_like(term)

    gate_mat = gate_w[...].reshape(-1, width)
    up_mat = up_w[...].reshape(-1, width)
    out_mat = out_w[...].reshape(-1, width)
    gate_pre = over_last(latent[...], gate_mat)
    up_pre = over_last(latent[...], up_mat)
    act_grad = over_last(routed[...], out_mat)
    sig = 1.0 / (1.0 + jnp.exp(-gate_pre))
    active = (gate_pre * sig * up_pre).astype(bf16).astype(f32)
    term[...] += jnp.sum(act_grad * active, axis=1, keepdims=True)
    gate_back = (act_grad * up_pre * sig * (1.0 + gate_pre * (1.0 - sig))).astype(bf16)
    up_back = (act_grad * gate_pre * sig).astype(bf16)
    block[...] += jnp.dot(gate_back, gate_mat, preferred_element_type=f32) + jnp.dot(
        up_back, up_mat, preferred_element_type=f32
    )

    @pl.when(step == pl.num_programs(0) - 1)
    def _():
        share = term[...] / jnp.where(gate > 0, gate, 1.0)
        gate_grad = jnp.where(marks[...] > 0, share, 0.0)
        keep[:, half:] = gate_grad
        send[:, half:] = gate_grad.astype(bf16)

        @pl.when(core[0] == 0)
        def _():
            keep[:, :half] = block[:, :half]
            send[:, :half] = block[:, half:].astype(bf16)

        @pl.when(core[0] != 0)
        def _():
            keep[:, :half] = block[:, half:]
            send[:, :half] = block[:, :half].astype(bf16)


def whole(shape):
    return pl.BlockSpec(shape, lambda i, core: (0,) * len(shape))


def call(kernel, name, scalar, args, in_specs, out_specs, out_shape, steps, mib, scratch=(), cost=None):
    return pl.pallas_call(
        kernel,
        grid_spec=pltpu.PrefetchScalarGridSpec(
            num_scalar_prefetch=1,
            grid=(steps,),
            in_specs=in_specs,
            out_specs=out_specs,
            scratch_shapes=list(scratch),
        ),
        out_shape=out_shape,
        compiler_params=limit(mib),
        cost_estimate=cost,
        name=name,
    )(scalar, *args)


def struct(shape, dtype):
    return jax.ShapeDtypeStruct(shape, dtype)


def call_head(core, own, peer, gain, words, target):
    rows = own.shape[0]
    places, _, cols, count = words.shape
    steps, _, span = gain.shape
    half = steps // 2

    def part(i, core):
        return (i % half, jnp.where(i < half, core[0], 1 - core[0]), 0, 0)

    return call(
        head_kernel,
        "head",
        core,
        (own, peer, gain, words, target),
        [
            whole(own.shape),
            whole(peer.shape),
            pl.BlockSpec((1, 1, span), lambda i, core: (i, 0, 0)),
            pl.BlockSpec((span // cols, 1, cols, count), part),
            whole(target.shape),
        ],
        [whole((rows, count)), whole((8, 128)), whole((rows, 128))],
        [struct((rows, count), f32), struct((8, 128), f32), struct((rows, 128), f32)],
        steps,
        24,
    )


def call_loss(core, stats, logits, target, cot, scale, words, per):
    places, _, cols, count = words.shape
    rows = logits.shape[0]
    return call(
        loss_kernel,
        "loss",
        core,
        (stats, logits, target, cot, scale, words),
        [
            whole(stats.shape),
            whole(logits.shape),
            whole(target.shape),
            whole(cot.shape),
            whole(scale.shape),
            pl.BlockSpec((per, 1, cols, count), lambda i, core: (i, 1 - core[0], 0, 0)),
        ],
        [
            whole((rows, count)),
            pl.BlockSpec((rows, per * cols), lambda i, core: (0, i)),
            whole((8, rows)),
            whole((rows, 128)),
        ],
        [
            struct((rows, count), bf16),
            struct((rows, places * cols), bf16),
            struct((8, rows), f32),
            struct((rows, 128), f32),
        ],
        places // per,
        24,
    )


def call_keep(core, grad, words, per):
    places, _, cols, count = words.shape
    rows = grad.shape[0]
    return call(
        keep_kernel,
        "keep",
        core,
        (grad, words),
        [
            whole(grad.shape),
            pl.BlockSpec((per, 1, cols, count), lambda i, core: (i, core[0], 0, 0)),
        ],
        pl.BlockSpec((rows, per * cols), lambda i, core: (0, i)),
        struct((rows, places * cols), f32),
        places // per,
        24,
        cost=pl.CostEstimate(
            flops=places * cols * rows * count * 2,
            bytes_accessed=places * cols * count * 2,
            transcendentals=0,
        ),
    )


def call_lower(place, parts, hidden, gain, marks, lift):
    places, chunk, wide = parts.shape
    width = lift.shape[1]
    cols = wide // places
    return call(
        lower_kernel,
        "lower",
        place,
        (parts, hidden, gain, marks, lift),
        [
            whole(parts.shape),
            whole(hidden.shape),
            whole(gain.shape),
            pl.BlockSpec((chunk, 128), lambda i, place: (place[0], 0)),
            whole(lift.shape),
        ],
        [whole((places, chunk, 2 * cols)), whole((chunk, width))],
        [struct((places, chunk, 2 * cols), bf16), struct((chunk, width), f32)],
        1,
        24,
    )


def call_expert(core, own, peer, latent, marks, weights):
    rows, width = latent.shape
    quarters, _, units, _ = weights.shape
    lanes = own.shape[1] + marks.shape[1]
    per = 2

    def part(k):
        return pl.BlockSpec((per, 1, units, width), lambda i, core: (i, k, 0, 0))

    return call(
        expert_kernel,
        "expert",
        core,
        (own, peer, latent, marks, weights, weights, weights),
        [
            whole(own.shape),
            whole(peer.shape),
            whole(latent.shape),
            whole(marks.shape),
            part(0),
            part(1),
            part(2),
        ],
        [whole((rows, lanes)), whole((rows, lanes))],
        [struct((rows, lanes), f32), struct((rows, lanes), bf16)],
        quarters // per,
        56,
        scratch=[
            pltpu.VMEM((rows, width), bf16),
            pltpu.VMEM((rows, width), f32),
            pltpu.VMEM((rows, 1), f32),
        ],
    )


def on_device(
    latent,
    residual,
    gates,
    route_ids,
    w_gate,
    w_up,
    w_out,
    w_lift,
    norm_gain,
    w_vocab,
    targets,
    loss_cot,
):
    core = lax.axis_index("c")
    own_index = lax.axis_index(slab)
    place = lax.axis_index(plane)
    places = lax.axis_size(plane)
    groups = lax.axis_size("dp")
    rows, width = latent.shape
    half = width // 2
    cols = residual.shape[1]
    words = w_vocab.shape[1]
    chunk = rows // places
    wide = places * cols
    first = core == 0

    def mine(x, axis):
        a, b = jnp.split(x, 2, axis)
        return jnp.where(first, a, b)

    def other(x, axis):
        a, b = jnp.split(x, 2, axis)
        return jnp.where(first, b, a)

    def joined(own, peer, axis):
        return jnp.where(
            first,
            jnp.concatenate([own, peer], axis),
            jnp.concatenate([peer, own], axis),
        )

    gate_mat, up_mat, out_mat = w_gate[0], w_up[0], w_out[0]
    lift_wide = lax.all_gather(w_lift.T, plane, axis=0, tiled=True)

    chosen = route_ids == own_index
    gate_own = jnp.sum(jnp.where(chosen, gates, 0.0), axis=1)
    high = lax.reduce_precision(gate_own, 8, 7)
    middle = lax.reduce_precision(gate_own - high, 8, 7)
    low = gate_own - high - middle
    gate_rows = jnp.concatenate([high, middle, low, jnp.zeros_like(low)]).reshape(-1, half)
    extra = jnp.pad(gate_rows.astype(bf16), ((0, 16 - gate_rows.shape[0]), (0, 0)))
    out_keep = mine(out_mat, 1)
    out_peer = swap(other(out_mat, 1))

    lat_own = spread(jnp.concatenate([mine(latent, 1), extra]), "dp")
    lat_peer = swap(lat_own)

    def gate_of(x):
        parts = x[:, rows : rows + gate_rows.shape[0]].reshape(groups, -1).astype(f32)
        parts = parts.reshape(groups, -1, rows)
        return (parts[:, 0] + parts[:, 1] + parts[:, 2]).reshape(-1)

    gate_all, gate_peer = gate_of(lat_own), gate_of(lat_peer)
    lat_all = joined(lat_own[:, :rows], lat_peer[:, :rows], 2).reshape(-1, width)
    gate_part = dot(lat_all, gate_mat, 1, 0)
    up_part = dot(lat_all, up_mat, 1, 0)
    active = (jax.nn.silu(gate_part) * up_part).astype(bf16)
    active_peer = swap(active)
    part = dot(active, out_keep, 1, 0) * gate_all[:, None]
    part = part + dot(active_peer, out_peer, 1, 0) * gate_peer[:, None]
    summed = jnp.sum(deal(part, "dp").reshape(groups, rows, half), axis=0)

    summed = summed.reshape(places, chunk, half)
    carried = residual.reshape(places, chunk, cols).astype(f32)
    carried = jnp.pad(carried, ((0, 0), (0, 0), (0, 128 - cols)))
    dealt = deal(jnp.concatenate([summed, carried], axis=2), plane)
    comb_own = jnp.sum(dealt[:, :, :half], axis=0).astype(bf16)
    res_rows = dealt[:, :, half : half + cols].transpose(1, 0, 2).reshape(chunk, wide)
    comb_own, gate_mat, up_mat, out_mat = lax.optimization_barrier(
        (comb_own, gate_mat, up_mat, out_mat)
    )
    weights = lax.all_gather(jnp.stack([gate_mat.T, up_mat.T, out_mat]), "dp")

    combined = joined(comb_own, swap(comb_own), 1)
    hidden = (res_rows + dot(combined, lift_wide, 1, 1)).astype(bf16)
    hid_own = spread(hidden, plane).reshape(rows, wide)

    per = 16
    steps = places // per
    core_id = core.astype(jnp.int32)[None]
    gain_sides = norm_gain.astype(f32).reshape(places, 2, cols)
    gain_own = jnp.where(first, gain_sides[:, 0], gain_sides[:, 1]).reshape(steps, 1, -1)
    gain_peer = jnp.where(first, gain_sides[:, 1], gain_sides[:, 0]).reshape(steps, 1, -1)
    target = (targets - own_index * words)[:, None]
    vocab = w_vocab.reshape(places, 2, cols, words)
    logits, stats, scale = call_head(
        core_id, hid_own, swap(hid_own), jnp.concatenate([gain_own, gain_peer]), vocab, target
    )
    stats_all = spread(stats, slab)
    grad, send, loss, marks = call_loss(
        core_id, stats_all, logits, target, loss_cot[None], scale, vocab, 8
    )
    row_loss = loss[0]
    keep = call_keep(core_id, grad, vocab, 8)
    keep = (keep + swap(send).astype(f32)).astype(bf16)
    parts = deal(keep.reshape(places, chunk, wide), plane)
    chunks, partial = call_lower(
        place.astype(jnp.int32)[None], parts, hidden, gain_own.reshape(1, wide), marks, lift_wide
    )
    cg_rows = (mine(partial, 1) + swap(other(partial, 1))).astype(bf16)
    cg_rows = jnp.broadcast_to(cg_rows[None], (places, chunk, half))
    dealt = deal(jnp.concatenate([cg_rows, chunks], axis=2), plane)
    cg_own = dealt[:, :, :half].reshape(rows, half)
    d_residual = dealt[:, :, half : half + cols].astype(f32) + dealt[:, :, half + cols :].astype(f32)
    d_residual = d_residual.reshape(rows, cols)

    gate_marks = jnp.where(chosen, gates, 0.0)
    gate_marks = jnp.pad(gate_marks, ((0, 0), (0, 128 - gate_marks.shape[1])))
    keep, send = call_expert(core_id, cg_own, swap(cg_own), latent, gate_marks, weights)
    keep = (keep + swap(send).astype(f32)).astype(bf16)
    tail = jnp.sum(deal(keep, plane).astype(f32).reshape(places, chunk, -1), axis=0).astype(bf16)
    tail = spread(tail, plane).reshape(rows, -1)
    d_latent = joined(tail[:, :half], swap(tail[:, :half]), 1).astype(f32)
    d_gates = tail[:, half : half + gates.shape[1]].astype(f32)
    return (row_loss, d_residual, d_latent, d_gates)


def solution(mesh):
    fine = Mesh(mesh.devices.reshape(mesh.devices.shape[0], 8, 4, 2), ("dp", "z", "y", "c"))
    in_specs = (
        P("dp", None),
        P("dp", slab),
        P("dp", None),
        P("dp", None),
        P(slab, None, "dp"),
        P(slab, None, "dp"),
        P(slab, "dp", None),
        P(None, slab),
        P(),
        P(None, slab),
        P("dp"),
        P("dp"),
    )
    out_specs = (P("dp"), P("dp", slab), P("dp", None), P("dp", None))
    return jax.shard_map(
        on_device, mesh=fine, in_specs=in_specs, out_specs=out_specs, check_vma=False
    )
```

```python
import jax
import jax.numpy as jnp
from jax import lax
from jax.experimental import pallas as pl
from jax.experimental.pallas import tpu as pltpu
from jax.sharding import Mesh, PartitionSpec as P

norm_epsilon = 1e-05
plane = ("z", "y")
slab = ("z", "y", "c")
bf16 = jnp.bfloat16
f32 = jnp.float32


def dot(a, b, ca, cb):
    return lax.dot_general(a, b, (((ca,), (cb,)), ((), ())), preferred_element_type=f32)


def swap(x):
    return lax.ppermute(x, "c", [(0, 1), (1, 0)])


def deal(x, axes):
    return lax.all_to_all(x, axes, 0, 0, tiled=True)


def spread(x, axes):
    count = lax.axis_size(axes)
    return deal(jnp.broadcast_to(x[None], (count,) + x.shape), axes)


def limit(mib):
    return pltpu.CompilerParams(vmem_limit_bytes=mib << 20)


def over_last(x, w):
    return lax.dot_general(x, w, (((1,), (1,)), ((), ())), preferred_element_type=f32)


def head_kernel(core, own, peer, gain, words, target, logits, stats, scale):
    step = pl.program_id(0)
    last = pl.num_programs(0) - 1
    rows, wide = own.shape
    span = gain.shape[2]
    half = wide // span

    @pl.when(step == 0)
    def _():
        total = jnp.zeros((rows, 128), f32)
        for k in range(wide // 128):
            a = own[:, k * 128 : (k + 1) * 128].astype(f32)
            b = peer[:, k * 128 : (k + 1) * 128].astype(f32)
            total = total + a * a + b * b
        mean = jnp.sum(total, axis=1, keepdims=True) / (2 * wide) + norm_epsilon
        guess = lax.rsqrt(mean)
        guess = guess * (1.5 - 0.5 * mean * guess * guess)
        scale[...] = jnp.broadcast_to(guess, scale.shape)

    def add(source, index):
        h = source[:, pl.ds(pl.multiple_of(index * span, span), span)].astype(f32)
        h = (h * scale[:, 0:1] * gain[0]).astype(bf16)
        rhs = words[...].reshape(span, -1)
        part = jnp.dot(h, rhs, preferred_element_type=f32)

        @pl.when(step == 0)
        def _():
            logits[...] = part

        @pl.when(step > 0)
        def _():
            logits[...] += part

    @pl.when(step < half)
    def _():
        add(own, step)

    @pl.when(step >= half)
    def _():
        add(peer, step - half)

    @pl.when(step == last)
    def _():
        values = logits[...]
        peak = jnp.max(values, axis=1, keepdims=True)
        below = values - peak
        weight = jnp.exp(below)
        total = jnp.sum(weight, axis=1, keepdims=True)
        lean = jnp.sum(weight * below, axis=1, keepdims=True)
        at = lax.broadcasted_iota(jnp.int32, values.shape, 1) == target[...]
        hit = jnp.sum(jnp.where(at, values, 0.0), axis=1, keepdims=True)
        lane = lax.broadcasted_iota(jnp.int32, (rows, 128), 1)
        packed = jnp.where(lane == 0, peak, jnp.where(lane == 1, total, 0.0))
        packed = jnp.where(lane == 2, lean, jnp.where(lane == 3, hit, packed))
        packed = packed.T
        stats[0:4, :] = packed[0:4, 0:128]
        stats[4:8, :] = packed[0:4, 128:256]


def loss_kernel(core, stats, logits, target, cot, scale, words, grad, send, loss, marks):
    @pl.when(pl.program_id(0) == 0)
    def _():
        def stat(k):
            return jnp.concatenate([stats[:, k, :], stats[:, k + 4, :]], axis=1)

        peaks = stat(0)
        peak = jnp.max(peaks, axis=0, keepdims=True)
        gap = peaks - peak
        share = jnp.exp(gap)
        totals = stat(1)
        total = jnp.sum(share * totals, axis=0, keepdims=True)
        lean = jnp.sum(share * (stat(2) + gap * totals), axis=0, keepdims=True)
        hit = jnp.sum(stat(3), axis=0, keepdims=True)
        inverse = 1.0 / total
        inner = cot[...] * (lean * inverse - (hit - peak))
        row = lax.broadcasted_iota(jnp.int32, (128, peak.shape[1]), 0)
        packed = jnp.where(row == 0, peak, jnp.where(row == 1, inverse, 0.0))
        packed = jnp.where(row == 2, cot[...], jnp.where(row == 3, inner, packed))
        col = packed.T
        loss[...] = jnp.broadcast_to(peak + jnp.log(total) - hit, loss.shape)
        lane = lax.broadcasted_iota(jnp.int32, marks.shape, 1)
        marks[...] = jnp.where(lane == 0, scale[...], col[:, 3:4])
        probs = jnp.exp(logits[...] - col[:, 0:1]) * col[:, 1:2]
        at = lax.broadcasted_iota(jnp.int32, probs.shape, 1) == target[...]
        grad[...] = (col[:, 2:3] * (probs - jnp.where(at, 1.0, 0.0))).astype(bf16)

    rhs = words[...].reshape(-1, words.shape[3])
    send[...] = over_last(grad[...], rhs).astype(send.dtype)


def keep_kernel(core, grad, words, keep):
    keep[...] = over_last(grad[...], words[...].reshape(-1, words.shape[3]))


def lower_kernel(place, parts, hidden, gain, marks, lift, chunks, partial):
    total = jnp.sum(parts[...].astype(f32), axis=0)
    scale = marks[:, 0:1]
    inner = marks[:, 1:2]
    model = 2 * hidden.shape[1]
    d_res = scale * (total * gain[...])
    d_res = d_res - hidden[...].astype(f32) * (scale * scale * (inner / model))
    high = d_res.astype(bf16)
    low = (d_res - high.astype(f32)).astype(bf16)
    cols = chunks.shape[2] // 2
    for k in range(chunks.shape[0]):
        chunks[k, :, :cols] = high[:, k * cols : (k + 1) * cols]
        chunks[k, :, cols:] = low[:, k * cols : (k + 1) * cols]
    partial[...] = jnp.dot(high, lift[...], preferred_element_type=f32)


def expert_kernel(
    core, own, peer, latent_t, marks, gate_w, up_w, out_w, keep, send, routed_t, block, term
):
    step = pl.program_id(0)
    half = own.shape[1]
    width, rows = latent_t.shape
    gate = jnp.sum(marks[...], axis=1, keepdims=True)

    @pl.when(step == 0)
    def _():
        a = (own[...].astype(f32) * gate).T.astype(bf16)
        b = (peer[...].astype(f32) * gate).T.astype(bf16)

        @pl.when(core[0] == 0)
        def _():
            routed_t[:half, :] = a
            routed_t[half:, :] = b

        @pl.when(core[0] != 0)
        def _():
            routed_t[:half, :] = b
            routed_t[half:, :] = a

        block[...] = jnp.zeros_like(block)
        term[...] = jnp.zeros_like(term)

    gate_mat = gate_w[...].reshape(-1, width)
    up_mat = up_w[...].reshape(-1, width)
    out_mat = out_w[...].reshape(-1, width)
    gate_pre = jnp.dot(gate_mat, latent_t[...], preferred_element_type=f32)
    up_pre = jnp.dot(up_mat, latent_t[...], preferred_element_type=f32)
    act_grad = jnp.dot(out_mat, routed_t[...], preferred_element_type=f32)
    sig = 1.0 / (1.0 + jnp.exp(-gate_pre))
    silu = gate_pre * sig
    active = (silu * up_pre).astype(bf16).astype(f32)
    term[...] += jnp.sum(act_grad * active, axis=0, keepdims=True)
    gate_back = (act_grad * up_pre * sig * (1.0 + gate_pre * (1.0 - sig))).T.astype(bf16)
    up_back = (act_grad * silu).T.astype(bf16)
    block[...] += jnp.dot(gate_back, gate_mat, preferred_element_type=f32) + jnp.dot(
        up_back, up_mat, preferred_element_type=f32
    )

    @pl.when(step == pl.num_programs(0) - 1)
    def _():
        column = jnp.broadcast_to(term[...], (128, rows)).T[:, 0:1]
        share = column / jnp.where(gate > 0, gate, 1.0)
        gate_grad = jnp.where(marks[...] > 0, share, 0.0)
        keep[:, half:] = gate_grad
        send[:, half:] = gate_grad.astype(bf16)

        @pl.when(core[0] == 0)
        def _():
            keep[:, :half] = block[:, :half]
            send[:, :half] = block[:, half:].astype(bf16)

        @pl.when(core[0] != 0)
        def _():
            keep[:, :half] = block[:, half:]
            send[:, :half] = block[:, :half].astype(bf16)


def whole(shape):
    return pl.BlockSpec(shape, lambda i, core: (0,) * len(shape))


def call(kernel, name, scalar, args, in_specs, out_specs, out_shape, steps, mib, scratch=(), cost=None):
    return pl.pallas_call(
        kernel,
        grid_spec=pltpu.PrefetchScalarGridSpec(
            num_scalar_prefetch=1,
            grid=(steps,),
            in_specs=in_specs,
            out_specs=out_specs,
            scratch_shapes=list(scratch),
        ),
        out_shape=out_shape,
        compiler_params=limit(mib),
        cost_estimate=cost,
        name=name,
    )(scalar, *args)


def struct(shape, dtype):
    return jax.ShapeDtypeStruct(shape, dtype)


def call_head(core, own, peer, gain, words, target):
    rows = own.shape[0]
    places, _, cols, count = words.shape
    steps, _, span = gain.shape
    half = steps // 2

    def part(i, core):
        return (i % half, jnp.where(i < half, core[0], 1 - core[0]), 0, 0)

    return call(
        head_kernel,
        "head",
        core,
        (own, peer, gain, words, target),
        [
            whole(own.shape),
            whole(peer.shape),
            pl.BlockSpec((1, 1, span), lambda i, core: (i, 0, 0)),
            pl.BlockSpec((span // cols, 1, cols, count), part),
            whole(target.shape),
        ],
        [whole((rows, count)), whole((8, 128)), whole((rows, 128))],
        [struct((rows, count), f32), struct((8, 128), f32), struct((rows, 128), f32)],
        steps,
        57,
    )


def call_loss(core, stats, logits, target, cot, scale, words, per):
    places, _, cols, count = words.shape
    rows = logits.shape[0]
    return call(
        loss_kernel,
        "loss",
        core,
        (stats, logits, target, cot, scale, words),
        [
            whole(stats.shape),
            whole(logits.shape),
            whole(target.shape),
            whole(cot.shape),
            whole(scale.shape),
            pl.BlockSpec((per, 1, cols, count), lambda i, core: (i, 1 - core[0], 0, 0)),
        ],
        [
            whole((rows, count)),
            pl.BlockSpec((rows, per * cols), lambda i, core: (0, i)),
            whole((8, rows)),
            whole((rows, 128)),
        ],
        [
            struct((rows, count), bf16),
            struct((rows, places * cols), bf16),
            struct((8, rows), f32),
            struct((rows, 128), f32),
        ],
        places // per,
        57,
    )


def call_keep(core, grad, words, per):
    places, _, cols, count = words.shape
    rows = grad.shape[0]
    return call(
        keep_kernel,
        "keep",
        core,
        (grad, words),
        [
            whole(grad.shape),
            pl.BlockSpec((per, 1, cols, count), lambda i, core: (i, core[0], 0, 0)),
        ],
        pl.BlockSpec((rows, per * cols), lambda i, core: (0, i)),
        struct((rows, places * cols), f32),
        places // per,
        57,
        cost=pl.CostEstimate(
            flops=places * cols * rows * count * 2,
            bytes_accessed=places * cols * count * 2,
            transcendentals=0,
        ),
    )


def call_lower(place, parts, hidden, gain, marks, lift):
    places, chunk, wide = parts.shape
    width = lift.shape[1]
    cols = wide // places
    return call(
        lower_kernel,
        "lower",
        place,
        (parts, hidden, gain, marks, lift),
        [
            whole(parts.shape),
            whole(hidden.shape),
            whole(gain.shape),
            pl.BlockSpec((chunk, 128), lambda i, place: (place[0], 0)),
            whole(lift.shape),
        ],
        [whole((places, chunk, 2 * cols)), whole((chunk, width))],
        [struct((places, chunk, 2 * cols), bf16), struct((chunk, width), f32)],
        1,
        60,
    )


def call_expert(core, own, peer, latent_t, marks, weights):
    width, rows = latent_t.shape
    quarters, _, units, _ = weights.shape
    lanes = own.shape[1] + marks.shape[1]
    per = 2

    def part(k):
        return pl.BlockSpec((per, 1, units, width), lambda i, core: (i, k, 0, 0))

    return call(
        expert_kernel,
        "expert",
        core,
        (own, peer, latent_t, marks, weights, weights, weights),
        [
            whole(own.shape),
            whole(peer.shape),
            whole(latent_t.shape),
            whole(marks.shape),
            part(0),
            part(1),
            part(2),
        ],
        [whole((rows, lanes)), whole((rows, lanes))],
        [struct((rows, lanes), f32), struct((rows, lanes), bf16)],
        quarters // per,
        58,
        scratch=[
            pltpu.VMEM((width, rows), bf16),
            pltpu.VMEM((rows, width), f32),
            pltpu.VMEM((1, rows), f32),
        ],
    )


def on_device(
    latent,
    residual,
    gates,
    route_ids,
    w_gate,
    w_up,
    w_out,
    w_lift,
    norm_gain,
    w_vocab,
    targets,
    loss_cot,
):
    core = lax.axis_index("c")
    own_index = lax.axis_index(slab)
    place = lax.axis_index(plane)
    places = lax.axis_size(plane)
    groups = lax.axis_size("dp")
    rows, width = latent.shape
    half = width // 2
    cols = residual.shape[1]
    words = w_vocab.shape[1]
    chunk = rows // places
    wide = places * cols
    first = core == 0

    def mine(x, axis):
        a, b = jnp.split(x, 2, axis)
        return jnp.where(first, a, b)

    def other(x, axis):
        a, b = jnp.split(x, 2, axis)
        return jnp.where(first, b, a)

    def joined(own, peer, axis):
        return jnp.where(
            first,
            jnp.concatenate([own, peer], axis),
            jnp.concatenate([peer, own], axis),
        )

    gate_mat, up_mat, out_mat = w_gate[0], w_up[0], w_out[0]
    lift_wide = lax.all_gather(w_lift.T[None], "z", axis=0, tiled=True)
    lift_wide = lax.all_gather(lift_wide, "y", axis=1, tiled=True).reshape(wide, width)

    chosen = route_ids == own_index
    gate_own = jnp.sum(jnp.where(chosen, gates, 0.0), axis=1)
    high = lax.reduce_precision(gate_own, 8, 7)
    middle = lax.reduce_precision(gate_own - high, 8, 7)
    low = gate_own - high - middle
    gate_rows = jnp.concatenate([high, middle, low, jnp.zeros_like(low)]).reshape(-1, half)
    extra = jnp.pad(gate_rows.astype(bf16), ((0, 16 - gate_rows.shape[0]), (0, 0)))
    out_keep = mine(out_mat, 1)
    out_peer = swap(other(out_mat, 1))

    lat_own = spread(jnp.concatenate([mine(latent, 1), extra]), "dp")
    lat_peer = swap(lat_own)

    def gate_of(x):
        parts = x[:, rows : rows + gate_rows.shape[0]].reshape(groups, -1).astype(f32)
        parts = parts.reshape(groups, -1, rows)
        return (parts[:, 0] + parts[:, 1] + parts[:, 2]).reshape(-1)

    gate_all, gate_peer = gate_of(lat_own), gate_of(lat_peer)
    lat_all = joined(lat_own[:, :rows], lat_peer[:, :rows], 2).reshape(-1, width)
    gate_part = dot(lat_all, gate_mat, 1, 0)
    up_part = dot(lat_all, up_mat, 1, 0)
    active = (jax.nn.silu(gate_part) * up_part).astype(bf16)
    active_peer = swap(active)
    part = dot(active, out_keep, 1, 0) * gate_all[:, None]
    part = part + dot(active_peer, out_peer, 1, 0) * gate_peer[:, None]
    part, gate_mat, up_mat, out_mat = lax.optimization_barrier((part, gate_mat, up_mat, out_mat))
    summed = jnp.sum(deal(part, "dp").reshape(groups, rows, half), axis=0)

    summed = summed.reshape(places, chunk, half)
    carried = residual.reshape(places, chunk, cols).astype(f32)
    carried = jnp.pad(carried, ((0, 0), (0, 0), (0, 128 - cols)))
    dealt = deal(jnp.concatenate([summed, carried], axis=2), plane)
    comb_own = jnp.sum(dealt[:, :, :half], axis=0).astype(bf16)
    res_rows = dealt[:, :, half : half + cols].transpose(1, 0, 2).reshape(chunk, wide)
    weights = lax.all_gather(jnp.stack([gate_mat.T, up_mat.T, out_mat]), "dp")

    combined = joined(comb_own, swap(comb_own), 1)
    hidden = (res_rows + dot(combined, lift_wide, 1, 1)).astype(bf16)
    hid_own = spread(hidden, plane).reshape(rows, wide)

    per = 16
    steps = places // per
    core_id = core.astype(jnp.int32)[None]
    gain_sides = norm_gain.astype(f32).reshape(places, 2, cols)
    gain_own = jnp.where(first, gain_sides[:, 0], gain_sides[:, 1]).reshape(steps, 1, -1)
    gain_peer = jnp.where(first, gain_sides[:, 1], gain_sides[:, 0]).reshape(steps, 1, -1)
    target = (targets - own_index * words)[:, None]
    vocab = w_vocab.reshape(places, 2, cols, words)
    logits, stats, scale = call_head(
        core_id, hid_own, swap(hid_own), jnp.concatenate([gain_own, gain_peer]), vocab, target
    )
    stats_all = spread(stats, slab)
    grad, send, loss, marks = call_loss(
        core_id, stats_all, logits, target, loss_cot[None], scale, vocab, 8
    )
    row_loss = loss[0]
    keep = call_keep(core_id, grad, vocab, 8)
    keep = (keep + swap(send).astype(f32)).astype(bf16)
    parts = deal(keep.reshape(places, chunk, wide), plane)
    chunks, partial = call_lower(
        place.astype(jnp.int32)[None], parts, hidden, gain_own.reshape(1, wide), marks, lift_wide
    )
    cg_rows = (mine(partial, 1) + swap(other(partial, 1))).astype(bf16)
    cg_rows = jnp.broadcast_to(cg_rows[None], (places, chunk, half))
    dealt = deal(jnp.concatenate([cg_rows, chunks], axis=2), plane)
    cg_own = dealt[:, :, :half].reshape(rows, half)
    d_residual = dealt[:, :, half : half + cols].astype(f32) + dealt[:, :, half + cols :].astype(f32)
    d_residual = d_residual.reshape(rows, cols)

    gate_marks = jnp.where(chosen, gates, 0.0)
    gate_marks = jnp.pad(gate_marks, ((0, 0), (0, 128 - gate_marks.shape[1])))
    keep, send = call_expert(core_id, cg_own, swap(cg_own), latent.T, gate_marks, weights)
    keep = (keep + swap(send).astype(f32)).astype(bf16)
    tail = jnp.sum(deal(keep, plane).astype(f32).reshape(places, chunk, -1), axis=0).astype(bf16)
    tail = spread(tail, plane).reshape(rows, -1)
    d_latent = joined(tail[:, :half], swap(tail[:, :half]), 1).astype(f32)
    d_gates = tail[:, half : half + gates.shape[1]].astype(f32)
    return (row_loss, d_residual, d_latent, d_gates)


def solution(mesh):
    fine = Mesh(mesh.devices.reshape(mesh.devices.shape[0], 8, 4, 2), ("dp", "z", "y", "c"))
    in_specs = (
        P("dp", None),
        P("dp", slab),
        P("dp", None),
        P("dp", None),
        P(slab, None, "dp"),
        P(slab, None, "dp"),
        P(slab, "dp", None),
        P(None, slab),
        P(),
        P(None, slab),
        P("dp"),
        P("dp"),
    )
    out_specs = (P("dp"), P("dp", slab), P("dp", None), P("dp", None))
    return jax.shard_map(
        on_device, mesh=fine, in_specs=in_specs, out_specs=out_specs, check_vma=False
    )
```

```python
import jax
import jax.numpy as jnp
from jax import lax
from jax.experimental import pallas as pl
from jax.experimental.pallas import tpu as pltpu
from jax.sharding import Mesh, PartitionSpec as P

norm_epsilon = 1e-05
plane = ("z", "y")
slab = ("z", "y", "c")
bf16 = jnp.bfloat16
f32 = jnp.float32


def dot(a, b, ca, cb):
    return lax.dot_general(a, b, (((ca,), (cb,)), ((), ())), preferred_element_type=f32)


def swap(x):
    return lax.ppermute(x, "c", [(0, 1), (1, 0)])


def deal(x, axes):
    return lax.all_to_all(x, axes, 0, 0, tiled=True)


def spread(x, axes):
    count = lax.axis_size(axes)
    return deal(jnp.broadcast_to(x[None], (count,) + x.shape), axes)


def over_last(x, w):
    return lax.dot_general(x, w, (((1,), (1,)), ((), ())), preferred_element_type=f32)


def bring(source, buffers, sems, count):
    copies = [pltpu.make_async_copy(source(k), buffers(k), sems.at[k]) for k in range(count)]
    for copy in copies:
        copy.start()
    return lambda k: copies[k].wait()


def head_kernel(core, own, peer, gain, words, target, logits, stats, scale, held, sems):
    rows, wide = own.shape
    blocks, per, cols, count = held.shape
    span = per * cols
    half = wide // span

    def source(k):
        side = core[0] if k < half else 1 - core[0]
        return words.at[pl.ds(k % half * per, per), side]

    wait = bring(source, lambda k: held.at[k], sems, blocks)
    total = jnp.zeros((rows, 128), f32)
    for k in range(wide // 128):
        a = own[:, k * 128 : (k + 1) * 128].astype(f32)
        b = peer[:, k * 128 : (k + 1) * 128].astype(f32)
        total = total + a * a + b * b
    mean = jnp.sum(total, axis=1, keepdims=True) / (2 * wide) + norm_epsilon
    guess = lax.rsqrt(mean)
    guess = guess * (1.5 - 0.5 * mean * guess * guess)
    scale[...] = jnp.broadcast_to(guess, scale.shape)
    for k in range(blocks):
        side = own if k < half else peer
        at = k % half * span
        h = side[:, at : at + span].astype(f32)
        h = (h * guess * gain[k : k + 1]).astype(bf16)
        wait(k)
        part = jnp.dot(h, held[k].reshape(span, count), preferred_element_type=f32)
        logits[...] = part if k == 0 else logits[...] + part

    values = logits[...]
    peak = jnp.max(values, axis=1, keepdims=True)
    below = values - peak
    weight = jnp.exp(below)
    total = jnp.sum(weight, axis=1, keepdims=True)
    lean = jnp.sum(weight * below, axis=1, keepdims=True)
    at = lax.broadcasted_iota(jnp.int32, values.shape, 1) == target[...]
    hit = jnp.sum(jnp.where(at, values, 0.0), axis=1, keepdims=True)
    lane = lax.broadcasted_iota(jnp.int32, (rows, 128), 1)
    packed = jnp.where(lane == 0, peak, jnp.where(lane == 1, total, 0.0))
    packed = jnp.where(lane == 2, lean, jnp.where(lane == 3, hit, packed))
    packed = packed.T
    stats[0:4, :] = packed[0:4, 0:128]
    stats[4:8, :] = packed[0:4, 128:256]


def grad_blocks(core, side, grad, words, held, sems):
    blocks, per, cols, count = held.shape
    wait = bring(
        lambda k: words.at[pl.ds(k * per, per), side], lambda k: held.at[k], sems, blocks
    )

    def block(k):
        wait(k)
        return over_last(grad[...], held[k].reshape(per * cols, count))

    return block


def loss_kernel(
    core, stats, logits, target, cot, scale, words, grad, send, loss, marks, held, sems
):
    block = grad_blocks(core, 1 - core[0], grad, words, held, sems)

    def stat(k):
        return jnp.concatenate([stats[:, k, :], stats[:, k + 4, :]], axis=1)

    peaks = stat(0)
    peak = jnp.max(peaks, axis=0, keepdims=True)
    gap = peaks - peak
    share = jnp.exp(gap)
    totals = stat(1)
    total = jnp.sum(share * totals, axis=0, keepdims=True)
    lean = jnp.sum(share * (stat(2) + gap * totals), axis=0, keepdims=True)
    hit = jnp.sum(stat(3), axis=0, keepdims=True)
    inverse = 1.0 / total
    inner = cot[...] * (lean * inverse - (hit - peak))
    row = lax.broadcasted_iota(jnp.int32, (128, peak.shape[1]), 0)
    packed = jnp.where(row == 0, peak, jnp.where(row == 1, inverse, 0.0))
    packed = jnp.where(row == 2, cot[...], jnp.where(row == 3, inner, packed))
    col = packed.T
    loss[...] = jnp.broadcast_to(peak + jnp.log(total) - hit, loss.shape)
    lane = lax.broadcasted_iota(jnp.int32, marks.shape, 1)
    marks[...] = jnp.where(lane == 0, scale[...], col[:, 3:4])
    probs = jnp.exp(logits[...] - col[:, 0:1]) * col[:, 1:2]
    at = lax.broadcasted_iota(jnp.int32, probs.shape, 1) == target[...]
    grad[...] = (col[:, 2:3] * (probs - jnp.where(at, 1.0, 0.0))).astype(bf16)
    blocks, per, cols, _ = held.shape
    span = per * cols
    for k in range(blocks):
        send[:, k * span : (k + 1) * span] = block(k).astype(send.dtype)


def keep_kernel(core, grad, words, keep, held, sems):
    block = grad_blocks(core, core[0], grad, words, held, sems)
    blocks, per, cols, _ = held.shape
    span = per * cols
    for k in range(blocks):
        keep[:, k * span : (k + 1) * span] = block(k)


def lift_kernel(core, own, peer, residual, lift, hidden, joined, held, sems):
    blocks, span, _ = held.shape
    half = own.shape[1]
    wait = bring(
        lambda k: lift.at[pl.ds(k * span, span)], lambda k: held.at[k], sems, blocks
    )
    flip = core[0] != 0
    joined[:, :half] = jnp.where(flip, peer[...], own[...])
    joined[:, half:] = jnp.where(flip, own[...], peer[...])
    rows = joined[...].astype(bf16)
    for k in range(blocks):
        wait(k)
        at = slice(k * span, (k + 1) * span)
        hidden[:, at] = (residual[:, at] + over_last(rows, held[k])).astype(bf16)


def lower_kernel(place, parts, hidden, gain, marks, lift, chunks, partial, held, sems):
    blocks, span, _ = held.shape
    wait = bring(
        lambda k: lift.at[pl.ds(k * span, span)], lambda k: held.at[k], sems, blocks
    )
    total = jnp.sum(parts[...].astype(f32), axis=0)
    scale = marks[:, 0:1]
    inner = marks[:, 1:2]
    model = 2 * hidden.shape[1]
    d_res = scale * (total * gain[...])
    d_res = d_res - hidden[...].astype(f32) * (scale * scale * (inner / model))
    high = d_res.astype(bf16)
    low = (d_res - high.astype(f32)).astype(bf16)
    cols = chunks.shape[2] // 2
    for k in range(chunks.shape[0]):
        chunks[k, :, :cols] = high[:, k * cols : (k + 1) * cols]
        chunks[k, :, cols:] = low[:, k * cols : (k + 1) * cols]
    out = jnp.zeros(partial.shape, f32)
    for k in range(blocks):
        wait(k)
        out = out + jnp.dot(
            high[:, k * span : (k + 1) * span], held[k], preferred_element_type=f32
        )
    partial[...] = out


def expert_kernel(core, own, peer, latent_t, marks_t, weights, keep, send, routed_t, held, sems):
    half = own.shape[1]
    width, rows = latent_t.shape
    quarters, mats, units, _ = weights.shape
    per = 2
    span = per * units
    copies = quarters * mats
    wait = bring(
        lambda k: weights.at[k // mats, k % mats],
        lambda k: held.at[k % mats, pl.ds(k // mats * units, units)],
        sems,
        copies,
    )
    gate = jnp.sum(marks_t[...], axis=0, keepdims=True)
    a = (own[...].astype(f32).T * gate).astype(bf16)
    b = (peer[...].astype(f32).T * gate).astype(bf16)

    @pl.when(core[0] == 0)
    def _():
        routed_t[:half, :] = a
        routed_t[half:, :] = b

    @pl.when(core[0] != 0)
    def _():
        routed_t[:half, :] = b
        routed_t[half:, :] = a

    def over_first(x, w):
        return lax.dot_general(x, w, (((0,), (0,)), ((), ())), preferred_element_type=f32)

    term = jnp.zeros((1, rows), f32)
    block = jnp.zeros((rows, width), f32)
    for k in range(quarters // per):
        for j in range(k * per * mats, (k + 1) * per * mats):
            wait(j)
        at = pl.ds(k * span, span)
        gate_mat, up_mat, out_mat = held[0, at], held[1, at], held[2, at]
        gate_pre = jnp.dot(gate_mat, latent_t[...], preferred_element_type=f32)
        up_pre = jnp.dot(up_mat, latent_t[...], preferred_element_type=f32)
        act_grad = jnp.dot(out_mat, routed_t[...], preferred_element_type=f32)
        sig = 1.0 / (1.0 + jnp.exp(-gate_pre))
        silu = gate_pre * sig
        active = (silu * up_pre).astype(bf16).astype(f32)
        term = term + jnp.sum(act_grad * active, axis=0, keepdims=True)
        gate_back = (act_grad * up_pre * sig * (1.0 + gate_pre * (1.0 - sig))).astype(bf16)
        up_back = (act_grad * silu).astype(bf16)
        block = block + over_first(gate_back, gate_mat) + over_first(up_back, up_mat)

    share = term / jnp.where(gate > 0, gate, 1.0)
    gate_grad = jnp.where(marks_t[...] > 0, share, 0.0).T
    keep[:, half:] = gate_grad
    send[:, half:] = gate_grad.astype(bf16)
    flip = core[0] != 0
    keep[:, :half] = jnp.where(flip, block[:, half:], block[:, :half])
    send[:, :half] = jnp.where(flip, block[:, :half], block[:, half:]).astype(bf16)


def struct(shape, dtype):
    return jax.ShapeDtypeStruct(shape, dtype)


def call(kernel, name, scalar, args, hbm, out_shape, scratch, mib=28, flops=0, choose=None):
    def spec(k, x):
        if k in hbm:
            return pl.BlockSpec(memory_space=pltpu.HBM)
        if choose is not None and k == choose[0]:
            return pl.BlockSpec(*choose[1:])
        return pl.BlockSpec(x.shape, lambda i, core: (0,) * x.ndim)

    def out_spec(x):
        return pl.BlockSpec(x.shape, lambda i, core: (0,) * len(x.shape))

    cost = None
    if flops:
        cost = pl.CostEstimate(flops=flops, bytes_accessed=flops // 512, transcendentals=0)
    args = [
        pltpu.with_memory_space_constraint(x, pltpu.HBM) if k in hbm else x
        for k, x in enumerate(args)
    ]
    return pl.pallas_call(
        kernel,
        grid_spec=pltpu.PrefetchScalarGridSpec(
            num_scalar_prefetch=1,
            grid=(1,),
            in_specs=[spec(k, x) for k, x in enumerate(args)],
            out_specs=[out_spec(x) for x in out_shape],
            scratch_shapes=scratch,
        ),
        out_shape=out_shape,
        compiler_params=pltpu.CompilerParams(vmem_limit_bytes=mib << 20),
        cost_estimate=cost,
        name=name,
    )(scalar, *args)


def block_scratch(blocks, shape):
    return [pltpu.VMEM((blocks,) + shape, bf16), pltpu.SemaphoreType.DMA((blocks,))]


def call_head(core, own, peer, gain, words, target):
    rows = own.shape[0]
    places, _, cols, count = words.shape
    blocks = gain.shape[0]
    return call(
        head_kernel,
        "head",
        core,
        (own, peer, gain, words, target),
        (3,),
        [struct((rows, count), f32), struct((8, 128), f32), struct((rows, 128), f32)],
        block_scratch(blocks, (2 * places // blocks, cols, count)),
    )


def call_loss(core, stats, logits, target, cot, scale, words):
    places, _, cols, count = words.shape
    rows = logits.shape[0]
    return call(
        loss_kernel,
        "loss",
        core,
        (stats, logits, target, cot, scale, words),
        (5,),
        [
            struct((rows, count), bf16),
            struct((rows, places * cols), bf16),
            struct((8, rows), f32),
            struct((rows, 128), f32),
        ],
        block_scratch(4, (places // 4, cols, count)),
    )


def call_keep(core, grad, words):
    places, _, cols, count = words.shape
    rows = grad.shape[0]
    return call(
        keep_kernel,
        "keep",
        core,
        (grad, words),
        (1,),
        [struct((rows, places * cols), f32)],
        block_scratch(4, (places // 4, cols, count)),
        flops=places * cols * rows * count * 2,
    )[0]


def call_lift(core, own, peer, residual, lift):
    wide, width = lift.shape
    return call(
        lift_kernel,
        "lift",
        core,
        (own.astype(f32), peer.astype(f32), residual, lift),
        (3,),
        [struct(residual.shape, bf16)],
        [pltpu.VMEM((own.shape[0], width), f32)] + block_scratch(4, (wide // 4, width)),
    )[0]


def call_lower(place, parts, hidden, gain, marks, lift):
    places, chunk, wide = parts.shape
    width = lift.shape[1]
    return call(
        lower_kernel,
        "lower",
        place,
        (parts, hidden, gain, marks, lift),
        (4,),
        [struct((places, chunk, 2 * (wide // places)), bf16), struct((chunk, width), f32)],
        block_scratch(4, (wide // 4, width)),
        choose=(3, (chunk, 128), lambda i, place: (place[0], 0)),
    )


def call_expert(core, own, peer, latent_t, marks_t, weights):
    width, rows = latent_t.shape
    quarters, mats, units, _ = weights.shape
    lanes = own.shape[1] + marks_t.shape[0]
    return call(
        expert_kernel,
        "expert",
        core,
        (own, peer, latent_t, marks_t, weights),
        (4,),
        [struct((rows, lanes), f32), struct((rows, lanes), bf16)],
        [
            pltpu.VMEM((width, rows), bf16),
            pltpu.VMEM((mats, quarters * units, width), bf16),
            pltpu.SemaphoreType.DMA((quarters * mats,)),
        ],
    )


def on_device(
    latent,
    residual,
    gates,
    route_ids,
    w_gate,
    w_up,
    w_out,
    w_lift,
    norm_gain,
    w_vocab,
    targets,
    loss_cot,
):
    core = lax.axis_index("c")
    own_index = lax.axis_index(slab)
    place = lax.axis_index(plane)
    places = lax.axis_size(plane)
    groups = lax.axis_size("dp")
    rows, width = latent.shape
    half = width // 2
    cols = residual.shape[1]
    words = w_vocab.shape[1]
    chunk = rows // places
    wide = places * cols
    first = core == 0

    def mine(x, axis):
        a, b = jnp.split(x, 2, axis)
        return jnp.where(first, a, b)

    def other(x, axis):
        a, b = jnp.split(x, 2, axis)
        return jnp.where(first, b, a)

    def joined(own, peer, axis):
        return jnp.where(
            first,
            jnp.concatenate([own, peer], axis),
            jnp.concatenate([peer, own], axis),
        )

    gate_mat, up_mat, out_mat = w_gate[0], w_up[0], w_out[0]
    lift_wide = lax.all_gather(w_lift.T, plane, axis=0, tiled=True)

    gate_marks = jnp.where(route_ids.T == own_index, gates.T, 0.0)
    gate_own = jnp.sum(gate_marks, axis=0)
    high = lax.reduce_precision(gate_own, 8, 7)
    middle = lax.reduce_precision(gate_own - high, 8, 7)
    low = gate_own - high - middle
    gate_rows = jnp.concatenate([high, middle, low, jnp.zeros_like(low)]).reshape(-1, half)
    extra = jnp.pad(gate_rows.astype(bf16), ((0, 16 - gate_rows.shape[0]), (0, 0)))
    out_keep = mine(out_mat, 1)
    out_peer = swap(other(out_mat, 1))

    lat_own = spread(jnp.concatenate([mine(latent, 1), extra]), "dp")
    lat_peer = swap(lat_own)

    def gate_of(x):
        parts = x[:, rows : rows + gate_rows.shape[0]].reshape(groups, -1).astype(f32)
        parts = parts.reshape(groups, -1, rows)
        return (parts[:, 0] + parts[:, 1] + parts[:, 2]).reshape(-1)

    gate_all, gate_peer = gate_of(lat_own), gate_of(lat_peer)
    lat_all = joined(lat_own[:, :rows], lat_peer[:, :rows], 2).reshape(-1, width)
    gate_part = dot(lat_all, gate_mat, 1, 0)
    up_part = dot(lat_all, up_mat, 1, 0)
    active = (jax.nn.silu(gate_part) * up_part).astype(bf16)
    active_peer = swap(active)
    part = dot(active, out_keep, 1, 0) * gate_all[:, None]
    part = part + dot(active_peer, out_peer, 1, 0) * gate_peer[:, None]
    part, gate_mat, up_mat, out_mat = lax.optimization_barrier((part, gate_mat, up_mat, out_mat))
    summed = jnp.sum(deal(part, "dp").reshape(groups, rows, half), axis=0)

    summed = summed.reshape(places, chunk, half)
    carried = residual.reshape(places, chunk, cols).astype(f32)
    carried = jnp.pad(carried, ((0, 0), (0, 0), (0, 128 - cols)))
    dealt = deal(jnp.concatenate([summed, carried], axis=2), plane)
    comb_own = jnp.sum(dealt[:, :, :half], axis=0).astype(bf16)
    res_rows = dealt[:, :, half : half + cols].transpose(1, 0, 2).reshape(chunk, wide)
    weights = lax.all_gather(jnp.stack([gate_mat.T, up_mat.T, out_mat]), "dp")

    core_id = core.astype(jnp.int32)[None]
    hidden = call_lift(core_id, comb_own, swap(comb_own), res_rows, lift_wide)
    hid_own = spread(hidden, plane).reshape(rows, wide)

    steps = 2
    gain_sides = norm_gain.astype(f32).reshape(places, 2, cols)
    gain_own = jnp.where(first, gain_sides[:, 0], gain_sides[:, 1]).reshape(steps, -1)
    gain_peer = jnp.where(first, gain_sides[:, 1], gain_sides[:, 0]).reshape(steps, -1)
    target = (targets - own_index * words)[:, None]
    vocab = w_vocab.reshape(places, 2, cols, words)
    logits, stats, scale = call_head(
        core_id, hid_own, swap(hid_own), jnp.concatenate([gain_own, gain_peer]), vocab, target
    )
    stats_all = spread(stats, slab)
    grad, send, loss, marks = call_loss(
        core_id, stats_all, logits, target, loss_cot[None], scale, vocab
    )
    row_loss = loss[0]
    keep = call_keep(core_id, grad, vocab)
    keep = (keep + swap(send).astype(f32)).astype(bf16)
    parts = deal(keep.reshape(places, chunk, wide), plane)
    chunks, partial = call_lower(
        place.astype(jnp.int32)[None], parts, hidden, gain_own.reshape(1, wide), marks, lift_wide
    )
    cg_rows = (mine(partial, 1) + swap(other(partial, 1))).astype(bf16)
    cg_rows = jnp.broadcast_to(cg_rows[None], (places, chunk, half))
    dealt = deal(jnp.concatenate([cg_rows, chunks], axis=2), plane)
    cg_own = dealt[:, :, :half].reshape(rows, half)
    d_residual = dealt[:, :, half : half + cols].astype(f32) + dealt[:, :, half + cols :].astype(f32)
    d_residual = d_residual.reshape(rows, cols)

    gate_marks = jnp.pad(gate_marks, ((0, 128 - gate_marks.shape[0]), (0, 0)))
    keep, send = call_expert(core_id, cg_own, swap(cg_own), latent.T, gate_marks, weights)
    keep = (keep + swap(send).astype(f32)).astype(bf16)
    tail = jnp.sum(deal(keep, plane).astype(f32).reshape(places, chunk, -1), axis=0).astype(bf16)
    tail = spread(tail, plane).reshape(rows, -1)
    d_latent = joined(tail[:, :half], swap(tail[:, :half]), 1).astype(f32)
    d_gates = tail[:, half : half + gates.shape[1]].astype(f32)
    return (row_loss, d_residual, d_latent, d_gates)


def solution(mesh):
    fine = Mesh(mesh.devices.reshape(mesh.devices.shape[0], 8, 4, 2), ("dp", "z", "y", "c"))
    in_specs = (
        P("dp", None),
        P("dp", slab),
        P("dp", None),
        P("dp", None),
        P(slab, None, "dp"),
        P(slab, None, "dp"),
        P(slab, "dp", None),
        P(None, slab),
        P(),
        P(None, slab),
        P("dp"),
        P("dp"),
    )
    out_specs = (P("dp"), P("dp", slab), P("dp", None), P("dp", None))
    return jax.shard_map(
        on_device, mesh=fine, in_specs=in_specs, out_specs=out_specs, check_vma=False
    )
```

```python
import jax
import jax.numpy as jnp
from jax import lax
from jax.experimental import pallas as pl
from jax.experimental.pallas import tpu as pltpu
from jax.sharding import Mesh, PartitionSpec as P

norm_epsilon = 1e-05
plane = ("z", "y")
slab = ("z", "y", "c")
bf16 = jnp.bfloat16
f32 = jnp.float32


def dot(a, b, ca, cb):
    return lax.dot_general(a, b, (((ca,), (cb,)), ((), ())), preferred_element_type=f32)


def swap(x):
    return lax.ppermute(x, "c", [(0, 1), (1, 0)])


def deal(x, axes):
    return lax.all_to_all(x, axes, 0, 0, tiled=True)


def spread(x, axes):
    count = lax.axis_size(axes)
    return deal(jnp.broadcast_to(x[None], (count,) + x.shape), axes)


def over_last(x, w):
    return lax.dot_general(x, w, (((1,), (1,)), ((), ())), preferred_element_type=f32)


def bring(source, buffers, sems, count):
    copies = [pltpu.make_async_copy(source(k), buffers(k), sems.at[k]) for k in range(count)]
    for copy in copies:
        copy.start()
    return lambda k: copies[k].wait()


def head_kernel(core, own, peer, gain, words, target, logits, stats, scale, held, sems):
    rows, wide = own.shape
    blocks, per, cols, count = held.shape
    span = per * cols
    half = wide // span

    def source(k):
        side = core[0] if k < half else 1 - core[0]
        return words.at[pl.ds(k % half * per, per), side]

    wait = bring(source, lambda k: held.at[k], sems, blocks)
    total = jnp.zeros((rows, 128), f32)
    for k in range(wide // 128):
        a = own[:, k * 128 : (k + 1) * 128].astype(f32)
        b = peer[:, k * 128 : (k + 1) * 128].astype(f32)
        total = total + a * a + b * b
    mean = jnp.sum(total, axis=1, keepdims=True) / (2 * wide) + norm_epsilon
    guess = lax.rsqrt(mean)
    guess = guess * (1.5 - 0.5 * mean * guess * guess)
    scale[...] = jnp.broadcast_to(guess, scale.shape)
    for k in range(blocks):
        side = own if k < half else peer
        at = k % half * span
        h = side[:, at : at + span].astype(f32)
        h = (h * guess * gain[k : k + 1]).astype(bf16)
        wait(k)
        part = jnp.dot(h, held[k].reshape(span, count), preferred_element_type=f32)
        logits[...] = part if k == 0 else logits[...] + part

    values = logits[...]
    peak = jnp.max(values, axis=1, keepdims=True)
    below = values - peak
    weight = jnp.exp(below)
    total = jnp.sum(weight, axis=1, keepdims=True)
    lean = jnp.sum(weight * below, axis=1, keepdims=True)
    at = lax.broadcasted_iota(jnp.int32, values.shape, 1) == target[...]
    hit = jnp.sum(jnp.where(at, values, 0.0), axis=1, keepdims=True)
    lane = lax.broadcasted_iota(jnp.int32, (rows, 128), 1)
    packed = jnp.where(lane == 0, peak, jnp.where(lane == 1, total, 0.0))
    packed = jnp.where(lane == 2, lean, jnp.where(lane == 3, hit, packed))
    packed = packed.T
    stats[0:4, :] = packed[0:4, 0:128]
    stats[4:8, :] = packed[0:4, 128:256]


def grad_blocks(core, side, grad, words, held, sems):
    blocks, per, cols, count = held.shape
    wait = bring(
        lambda k: words.at[pl.ds(k * per, per), side], lambda k: held.at[k], sems, blocks
    )

    def block(k):
        wait(k)
        return over_last(grad[...], held[k].reshape(per * cols, count))

    return block


def loss_kernel(
    core, stats, logits, target, cot, scale, words, grad, send, loss, marks, held, sems
):
    block = grad_blocks(core, 1 - core[0], grad, words, held, sems)

    def stat(k):
        return jnp.concatenate([stats[:, k, :], stats[:, k + 4, :]], axis=1)

    peaks = stat(0)
    peak = jnp.max(peaks, axis=0, keepdims=True)
    gap = peaks - peak
    share = jnp.exp(gap)
    totals = stat(1)
    total = jnp.sum(share * totals, axis=0, keepdims=True)
    lean = jnp.sum(share * (stat(2) + gap * totals), axis=0, keepdims=True)
    hit = jnp.sum(stat(3), axis=0, keepdims=True)
    inverse = 1.0 / total
    inner = cot[...] * (lean * inverse - (hit - peak))
    row = lax.broadcasted_iota(jnp.int32, (128, peak.shape[1]), 0)
    packed = jnp.where(row == 0, peak, jnp.where(row == 1, inverse, 0.0))
    packed = jnp.where(row == 2, cot[...], jnp.where(row == 3, inner, packed))
    col = packed.T
    loss[...] = jnp.broadcast_to(peak + jnp.log(total) - hit, loss.shape)
    lane = lax.broadcasted_iota(jnp.int32, marks.shape, 1)
    marks[...] = jnp.where(lane == 0, scale[...], col[:, 3:4])
    probs = jnp.exp(logits[...] - col[:, 0:1]) * col[:, 1:2]
    at = lax.broadcasted_iota(jnp.int32, probs.shape, 1) == target[...]
    grad[...] = (col[:, 2:3] * (probs - jnp.where(at, 1.0, 0.0))).astype(bf16)
    blocks, per, cols, _ = held.shape
    span = per * cols
    for k in range(blocks):
        send[:, k * span : (k + 1) * span] = block(k).astype(send.dtype)


def keep_kernel(core, grad, words, keep, held, sems):
    block = grad_blocks(core, core[0], grad, words, held, sems)
    blocks, per, cols, _ = held.shape
    span = per * cols
    for k in range(blocks):
        keep[:, k * span : (k + 1) * span] = block(k)


def lift_kernel(core, own, peer, residual, lift, hidden, joined, held, sems):
    blocks, span, _ = held.shape
    half = own.shape[1]
    wait = bring(
        lambda k: lift.at[pl.ds(k * span, span)], lambda k: held.at[k], sems, blocks
    )
    flip = core[0] != 0
    joined[:, :half] = jnp.where(flip, peer[...], own[...])
    joined[:, half:] = jnp.where(flip, own[...], peer[...])
    rows = joined[...].astype(bf16)
    for k in range(blocks):
        wait(k)
        at = slice(k * span, (k + 1) * span)
        hidden[:, at] = (residual[:, at] + over_last(rows, held[k])).astype(bf16)


def lower_kernel(place, parts, hidden, gain, marks, lift, chunks, partial, held, sems):
    blocks, span, _ = held.shape
    wait = bring(
        lambda k: lift.at[pl.ds(k * span, span)], lambda k: held.at[k], sems, blocks
    )
    total = jnp.sum(parts[...].astype(f32), axis=0)
    scale = marks[:, 0:1]
    inner = marks[:, 1:2]
    model = 2 * hidden.shape[1]
    d_res = scale * (total * gain[...])
    d_res = d_res - hidden[...].astype(f32) * (scale * scale * (inner / model))
    high = d_res.astype(bf16)
    low = (d_res - high.astype(f32)).astype(bf16)
    cols = chunks.shape[2] // 2
    for k in range(chunks.shape[0]):
        chunks[k, :, :cols] = high[:, k * cols : (k + 1) * cols]
        chunks[k, :, cols:] = low[:, k * cols : (k + 1) * cols]
    out = jnp.zeros(partial.shape, f32)
    for k in range(blocks):
        wait(k)
        out = out + jnp.dot(
            high[:, k * span : (k + 1) * span], held[k], preferred_element_type=f32
        )
    partial[...] = out


def unit_blocks(weights, mats, held, sems):
    quarters, _, units, _ = weights.shape
    many = len(mats)
    return bring(
        lambda k: weights.at[k // many, mats[k % many]],
        lambda k: held.at[k % many, pl.ds(k // many * units, units)],
        sems,
        quarters * many,
    )


def prepare_kernel(core, latent_t, weights, slope, silu, active, held, sems):
    wait = unit_blocks(weights, (0, 1), held, sems)
    span = weights.shape[2] * 2
    for k in range(2):
        for j in range(4 * k, 4 * k + 4):
            wait(j)
        at = pl.ds(k * span, span)
        gate_pre = jnp.dot(held[0, at], latent_t[...], preferred_element_type=f32)
        up_pre = jnp.dot(held[1, at], latent_t[...], preferred_element_type=f32)
        sig = 1.0 / (1.0 + jnp.exp(-gate_pre))
        silu[at, :] = gate_pre * sig
        slope[at, :] = up_pre * sig * (1.0 + gate_pre * (1.0 - sig))
        active[at, :] = (gate_pre * sig * up_pre).astype(bf16)


def expert_kernel(
    core, own, peer, slope, silu, active, marks_t, weights, keep, send, routed_t, held, sems
):
    half = own.shape[1]
    width, rows = routed_t.shape
    span = weights.shape[2] * 2
    wait = unit_blocks(weights, (2, 0, 1), held, sems)
    gate = jnp.sum(marks_t[...], axis=0, keepdims=True)
    a = (own[...].astype(f32).T * gate).astype(bf16)
    b = (peer[...].astype(f32).T * gate).astype(bf16)

    @pl.when(core[0] == 0)
    def _():
        routed_t[:half, :] = a
        routed_t[half:, :] = b

    @pl.when(core[0] != 0)
    def _():
        routed_t[:half, :] = b
        routed_t[half:, :] = a

    def over_first(x, w):
        return lax.dot_general(x, w, (((0,), (0,)), ((), ())), preferred_element_type=f32)

    term = jnp.zeros((1, rows), f32)
    block = jnp.zeros((rows, width), f32)
    for k in range(2):
        for j in range(6 * k, 6 * k + 6):
            wait(j)
        at = pl.ds(k * span, span)
        act_grad = jnp.dot(held[0, at], routed_t[...], preferred_element_type=f32)
        term = term + jnp.sum(act_grad * active[at, :].astype(f32), axis=0, keepdims=True)
        gate_back = (act_grad * slope[at, :]).astype(bf16)
        up_back = (act_grad * silu[at, :]).astype(bf16)
        block = block + over_first(gate_back, held[1, at]) + over_first(up_back, held[2, at])

    share = term / jnp.where(gate > 0, gate, 1.0)
    gate_grad = jnp.where(marks_t[...] > 0, share, 0.0).T
    keep[:, half:] = gate_grad
    send[:, half:] = gate_grad.astype(bf16)
    flip = core[0] != 0
    keep[:, :half] = jnp.where(flip, block[:, half:], block[:, :half])
    send[:, :half] = jnp.where(flip, block[:, :half], block[:, half:]).astype(bf16)


def mix_kernel(spot, own, peer, keep, other, gates, out):
    groups = gates.shape[0] // 2
    rows = gates.shape[1]
    row = lax.broadcasted_iota(jnp.int32, (128, rows), 0)

    def over_first(x, w):
        return lax.dot_general(x, w, (((0,), (0,)), ((), ())), preferred_element_type=f32)

    for k in range(groups):
        at = slice(k * rows, (k + 1) * rows)
        back = lax.rem(spot[1] + groups - k, groups)
        gate = gates[pl.ds(back, 1), :]
        gate_peer = gates[pl.ds(groups + back, 1), :]
        col = jnp.where(row == 0, gate, gate_peer).T
        part = over_first(own[:, at], keep[...]) * col[:, 0:1]
        out[at, :] = part + over_first(peer[:, at], other[...]) * col[:, 1:2]


def struct(shape, dtype):
    return jax.ShapeDtypeStruct(shape, dtype)


def call(kernel, name, scalar, args, hbm, out_shape, scratch, mib=28, flops=0, choose=None):
    def spec(k, x):
        if k in hbm:
            return pl.BlockSpec(memory_space=pltpu.HBM)
        if choose is not None and k == choose[0]:
            return pl.BlockSpec(*choose[1:])
        return pl.BlockSpec(x.shape, lambda i, core: (0,) * x.ndim)

    def out_spec(x):
        return pl.BlockSpec(x.shape, lambda i, core: (0,) * len(x.shape))

    cost = None
    if flops:
        cost = pl.CostEstimate(flops=flops, bytes_accessed=flops // 512, transcendentals=0)
    args = [
        pltpu.with_memory_space_constraint(x, pltpu.HBM) if k in hbm else x
        for k, x in enumerate(args)
    ]
    return pl.pallas_call(
        kernel,
        grid_spec=pltpu.PrefetchScalarGridSpec(
            num_scalar_prefetch=1,
            grid=(1,),
            in_specs=[spec(k, x) for k, x in enumerate(args)],
            out_specs=[out_spec(x) for x in out_shape],
            scratch_shapes=scratch,
        ),
        out_shape=out_shape,
        compiler_params=pltpu.CompilerParams(vmem_limit_bytes=mib << 20),
        cost_estimate=cost,
        name=name,
    )(scalar, *args)


def block_scratch(blocks, shape):
    return [pltpu.VMEM((blocks,) + shape, bf16), pltpu.SemaphoreType.DMA((blocks,))]


def call_head(core, own, peer, gain, words, target):
    rows = own.shape[0]
    places, _, cols, count = words.shape
    blocks = gain.shape[0]
    return call(
        head_kernel,
        "head",
        core,
        (own, peer, gain, words, target),
        (3,),
        [struct((rows, count), f32), struct((8, 128), f32), struct((rows, 128), f32)],
        block_scratch(blocks, (2 * places // blocks, cols, count)),
    )


def call_loss(core, stats, logits, target, cot, scale, words):
    places, _, cols, count = words.shape
    rows = logits.shape[0]
    return call(
        loss_kernel,
        "loss",
        core,
        (stats, logits, target, cot, scale, words),
        (5,),
        [
            struct((rows, count), bf16),
            struct((rows, places * cols), bf16),
            struct((8, rows), f32),
            struct((rows, 128), f32),
        ],
        block_scratch(4, (places // 4, cols, count)),
    )


def call_keep(core, grad, words):
    places, _, cols, count = words.shape
    rows = grad.shape[0]
    return call(
        keep_kernel,
        "keep",
        core,
        (grad, words),
        (1,),
        [struct((rows, places * cols), f32)],
        block_scratch(4, (places // 4, cols, count)),
        flops=places * cols * rows * count * 2,
    )[0]


def call_lift(core, own, peer, residual, lift):
    wide, width = lift.shape
    return call(
        lift_kernel,
        "lift",
        core,
        (own.astype(f32), peer.astype(f32), residual, lift),
        (3,),
        [struct(residual.shape, bf16)],
        [pltpu.VMEM((own.shape[0], width), f32)] + block_scratch(4, (wide // 4, width)),
    )[0]


def call_lower(place, parts, hidden, gain, marks, lift):
    places, chunk, wide = parts.shape
    width = lift.shape[1]
    return call(
        lower_kernel,
        "lower",
        place,
        (parts, hidden, gain, marks, lift),
        (4,),
        [struct((places, chunk, 2 * (wide // places)), bf16), struct((chunk, width), f32)],
        block_scratch(4, (wide // 4, width)),
        choose=(3, (chunk, 128), lambda i, place: (place[0], 0)),
    )


def unit_scratch(weights, mats):
    quarters, _, units, width = weights.shape
    return [
        pltpu.VMEM((mats, quarters * units, width), bf16),
        pltpu.SemaphoreType.DMA((quarters * mats,)),
    ]


def call_prepare(core, latent_t, weights):
    width, rows = latent_t.shape
    quarters, _, units, _ = weights.shape
    shape = (quarters * units, rows)
    return call(
        prepare_kernel,
        "prepare",
        core,
        (latent_t, weights),
        (1,),
        [struct(shape, f32), struct(shape, f32), struct(shape, bf16)],
        unit_scratch(weights, 2),
        flops=4 * rows * width * quarters * units,
    )


def call_expert(core, own, peer, prepared, marks_t, weights):
    rows, half = own.shape
    lanes = half + marks_t.shape[0]
    return call(
        expert_kernel,
        "expert",
        core,
        (own, peer) + tuple(prepared) + (marks_t, weights),
        (6,),
        [struct((rows, lanes), f32), struct((rows, lanes), bf16)],
        [pltpu.VMEM((2 * half, rows), bf16)] + unit_scratch(weights, 3),
    )


def call_mix(core, own, peer, keep, other, gates):
    shape = (own.shape[1], keep.shape[1])
    return call(
        mix_kernel, "mix", core, (own, peer, keep, other, gates), (), [struct(shape, f32)], []
    )[0]


def on_device(
    latent,
    residual,
    gates,
    route_ids,
    w_gate,
    w_up,
    w_out,
    w_lift,
    norm_gain,
    w_vocab,
    targets,
    loss_cot,
):
    core = lax.axis_index("c")
    own_index = lax.axis_index(slab)
    place = lax.axis_index(plane)
    places = lax.axis_size(plane)
    groups = lax.axis_size("dp")
    rows, width = latent.shape
    half = width // 2
    cols = residual.shape[1]
    words = w_vocab.shape[1]
    chunk = rows // places
    wide = places * cols
    first = core == 0

    def mine(x, axis):
        a, b = jnp.split(x, 2, axis)
        return jnp.where(first, a, b)

    def other(x, axis):
        a, b = jnp.split(x, 2, axis)
        return jnp.where(first, b, a)

    def joined(own, peer, axis):
        return jnp.where(
            first,
            jnp.concatenate([own, peer], axis),
            jnp.concatenate([peer, own], axis),
        )

    gate_mat, up_mat, out_mat = w_gate[0], w_up[0], w_out[0]
    lift_t = w_lift.T
    ring = lax.axis_size("y")
    around = [lift_t] + [
        lax.ppermute(lift_t, "y", [((i + k) % ring, i) for i in range(ring)])
        for k in range(1, ring)
    ]

    gate_marks = jnp.where(route_ids.T == own_index, gates.T, 0.0)
    gate_own = jnp.sum(gate_marks, axis=0)
    ahead = [gate_own] + [
        lax.ppermute(gate_own, "dp", [(i, (i + k) % groups) for i in range(groups)])
        for k in range(1, groups)
    ]
    out_keep = mine(out_mat, 1)
    out_peer = swap(other(out_mat, 1))

    lat_own = spread(mine(latent, 1), "dp")
    *ahead, lat_own = lax.optimization_barrier((*ahead, lat_own))
    lat_peer = swap(lat_own)
    turn = (ring - lax.axis_index("y")) % ring
    *around, lat_own = lax.optimization_barrier((*around, lat_own))
    lift_deep = lax.dynamic_slice_in_dim(jnp.stack(around + around), turn, ring, 0)
    lift_wide = lax.all_gather(lift_deep, "z", axis=0, tiled=True).reshape(wide, width)

    lat_all = joined(lat_own, lat_peer, 2).reshape(-1, width)
    gate_part = dot(lat_all, gate_mat, 1, 0)
    up_part = dot(lat_all, up_mat, 1, 0)
    active = (jax.nn.silu(gate_part) * up_part).astype(bf16)
    core_id = core.astype(jnp.int32)[None]
    ahead = jnp.stack(ahead)
    gate_rows = jnp.concatenate([ahead, swap(ahead)])
    spot = jnp.stack([core, lax.axis_index("dp")]).astype(jnp.int32)
    active_t = active.T
    part = call_mix(spot, active_t, swap(active_t), out_keep, out_peer, gate_rows)
    part, gate_mat, up_mat, out_mat = lax.optimization_barrier((part, gate_mat, up_mat, out_mat))
    weights = jnp.stack([gate_mat.T, up_mat.T, out_mat])
    summed = jnp.sum(deal(part, "dp").reshape(groups, rows, half), axis=0)

    summed, weights = lax.optimization_barrier((summed, weights))
    weights = lax.all_gather(weights, "dp")

    summed = summed.reshape(places, chunk, half)
    carried = residual.reshape(places, chunk, cols).astype(f32)
    carried = jnp.pad(carried, ((0, 0), (0, 0), (0, 128 - cols)))
    dealt = deal(jnp.concatenate([summed, carried], axis=2), plane)
    comb_own = jnp.sum(dealt[:, :, :half], axis=0).astype(bf16)
    res_rows = dealt[:, :, half : half + cols].transpose(1, 0, 2).reshape(chunk, wide)
    hidden = call_lift(core_id, comb_own, swap(comb_own), res_rows, lift_wide)
    hid_own = spread(hidden, plane).reshape(rows, wide)

    steps = 2
    gain_sides = norm_gain.astype(f32).reshape(places, 2, cols)
    gain_own = jnp.where(first, gain_sides[:, 0], gain_sides[:, 1]).reshape(steps, -1)
    gain_peer = jnp.where(first, gain_sides[:, 1], gain_sides[:, 0]).reshape(steps, -1)
    target = (targets - own_index * words)[:, None]
    vocab = w_vocab.reshape(places, 2, cols, words)
    logits, stats, scale = call_head(
        core_id, hid_own, swap(hid_own), jnp.concatenate([gain_own, gain_peer]), vocab, target
    )
    stats_all = spread(stats, slab)
    grad, send, loss, marks = call_loss(
        core_id, stats_all, logits, target, loss_cot[None], scale, vocab
    )
    row_loss = loss[0]
    keep = call_keep(core_id, grad, vocab)
    keep = (keep + swap(send).astype(f32)).astype(bf16)
    parts = deal(keep.reshape(places, chunk, wide), plane)
    prepared = call_prepare(core_id, latent.T, weights)
    parts, *prepared = lax.optimization_barrier((parts, *prepared))
    chunks, partial = call_lower(
        place.astype(jnp.int32)[None], parts, hidden, gain_own.reshape(1, wide), marks, lift_wide
    )
    cg_rows = (mine(partial, 1) + swap(other(partial, 1))).astype(bf16)
    cg_rows = jnp.broadcast_to(cg_rows[None], (places, chunk, half))
    dealt = deal(jnp.concatenate([cg_rows, chunks], axis=2), plane)
    cg_own = dealt[:, :, :half].reshape(rows, half)
    d_residual = dealt[:, :, half : half + cols].astype(f32) + dealt[:, :, half + cols :].astype(f32)
    d_residual = d_residual.reshape(rows, cols)

    gate_marks = jnp.pad(gate_marks, ((0, 128 - gate_marks.shape[0]), (0, 0)))
    keep, send = call_expert(core_id, cg_own, swap(cg_own), prepared, gate_marks, weights)
    keep = (keep + swap(send).astype(f32)).astype(bf16)
    tail = jnp.sum(deal(keep, plane).astype(f32).reshape(places, chunk, -1), axis=0).astype(bf16)
    tail = spread(tail, plane).reshape(rows, -1)
    d_latent = joined(tail[:, :half], swap(tail[:, :half]), 1).astype(f32)
    d_gates = tail[:, half : half + gates.shape[1]].astype(f32)
    return (row_loss, d_residual, d_latent, d_gates)


def solution(mesh):
    fine = Mesh(mesh.devices.reshape(mesh.devices.shape[0], 8, 4, 2), ("dp", "z", "y", "c"))
    in_specs = (
        P("dp", None),
        P("dp", slab),
        P("dp", None),
        P("dp", None),
        P(slab, None, "dp"),
        P(slab, None, "dp"),
        P(slab, "dp", None),
        P(None, slab),
        P(),
        P(None, slab),
        P("dp"),
        P("dp"),
    )
    out_specs = (P("dp"), P("dp", slab), P("dp", None), P("dp", None))
    return jax.shard_map(
        on_device, mesh=fine, in_specs=in_specs, out_specs=out_specs, check_vma=False
    )
```

```python
import jax
import jax.numpy as jnp
from jax import lax
from jax.experimental import pallas as pl
from jax.experimental.pallas import tpu as pltpu
from jax.sharding import Mesh, PartitionSpec as P

norm_epsilon = 1e-05
plane = ("z", "y")
slab = ("z", "y", "c")
bf16 = jnp.bfloat16
f32 = jnp.float32


def dot(a, b, ca, cb):
    return lax.dot_general(a, b, (((ca,), (cb,)), ((), ())), preferred_element_type=f32)


def swap(x):
    return lax.ppermute(x, "c", [(0, 1), (1, 0)])


def deal(x, axes):
    return lax.all_to_all(x, axes, 0, 0, tiled=True)


def spread(x, axes):
    count = lax.axis_size(axes)
    return deal(jnp.broadcast_to(x[None], (count,) + x.shape), axes)


def over_last(x, w):
    return lax.dot_general(x, w, (((1,), (1,)), ((), ())), preferred_element_type=f32)


def bring(source, buffers, sems, count):
    copies = [pltpu.make_async_copy(source(k), buffers(k), sems.at[k]) for k in range(count)]
    for copy in copies:
        copy.start()
    return lambda k: copies[k].wait()


def head_kernel(core, own, peer, gain, words, target, logits, stats, scale, held, sems):
    rows, wide = own.shape
    blocks, per, cols, count = held.shape
    span = per * cols
    half = wide // span

    def source(k):
        side = core[0] if k < half else 1 - core[0]
        return words.at[pl.ds(k % half * per, per), side]

    wait = bring(source, lambda k: held.at[k], sems, blocks)
    total = jnp.zeros((rows, 128), f32)
    for k in range(wide // 128):
        a = own[:, k * 128 : (k + 1) * 128].astype(f32)
        b = peer[:, k * 128 : (k + 1) * 128].astype(f32)
        total = total + a * a + b * b
    mean = jnp.sum(total, axis=1, keepdims=True) / (2 * wide) + norm_epsilon
    guess = lax.rsqrt(mean)
    guess = guess * (1.5 - 0.5 * mean * guess * guess)
    scale[...] = jnp.broadcast_to(guess, scale.shape)
    for k in range(blocks):
        side = own if k < half else peer
        at = k % half * span
        h = side[:, at : at + span].astype(f32)
        h = (h * guess * gain[k : k + 1]).astype(bf16)
        wait(k)
        part = jnp.dot(h, held[k].reshape(span, count), preferred_element_type=f32)
        logits[...] = part if k == 0 else logits[...] + part

    values = logits[...]
    peak = jnp.max(values, axis=1, keepdims=True)
    below = values - peak
    weight = jnp.exp(below)
    total = jnp.sum(weight, axis=1, keepdims=True)
    lean = jnp.sum(weight * below, axis=1, keepdims=True)
    at = lax.broadcasted_iota(jnp.int32, values.shape, 1) == target[...]
    hit = jnp.sum(jnp.where(at, values, 0.0), axis=1, keepdims=True)
    lane = lax.broadcasted_iota(jnp.int32, (rows, 128), 1)
    packed = jnp.where(lane == 0, peak, jnp.where(lane == 1, total, 0.0))
    packed = jnp.where(lane == 2, lean, jnp.where(lane == 3, hit, packed))
    packed = packed.T
    stats[0:4, :] = packed[0:4, 0:128]
    stats[4:8, :] = packed[0:4, 128:256]


def grad_blocks(core, side, grad, words, held, sems):
    blocks, per, cols, count = held.shape
    wait = bring(
        lambda k: words.at[pl.ds(k * per, per), side], lambda k: held.at[k], sems, blocks
    )

    def block(k):
        wait(k)
        return over_last(grad[...], held[k].reshape(per * cols, count))

    return block


def loss_kernel(
    core, stats, logits, target, cot, scale, words, grad, send, loss, marks, held, sems
):
    block = grad_blocks(core, 1 - core[0], grad, words, held, sems)

    def stat(k):
        return jnp.concatenate([stats[:, k, :], stats[:, k + 4, :]], axis=1)

    peaks = stat(0)
    peak = jnp.max(peaks, axis=0, keepdims=True)
    gap = peaks - peak
    share = jnp.exp(gap)
    totals = stat(1)
    total = jnp.sum(share * totals, axis=0, keepdims=True)
    lean = jnp.sum(share * (stat(2) + gap * totals), axis=0, keepdims=True)
    hit = jnp.sum(stat(3), axis=0, keepdims=True)
    inverse = 1.0 / total
    inner = cot[...] * (lean * inverse - (hit - peak))
    row = lax.broadcasted_iota(jnp.int32, (128, peak.shape[1]), 0)
    packed = jnp.where(row == 0, peak, jnp.where(row == 1, inverse, 0.0))
    packed = jnp.where(row == 2, cot[...], jnp.where(row == 3, inner, packed))
    col = packed.T
    loss[...] = jnp.broadcast_to(peak + jnp.log(total) - hit, loss.shape)
    lane = lax.broadcasted_iota(jnp.int32, marks.shape, 1)
    marks[...] = jnp.where(lane == 0, scale[...], col[:, 3:4])
    probs = jnp.exp(logits[...] - col[:, 0:1]) * col[:, 1:2]
    at = lax.broadcasted_iota(jnp.int32, probs.shape, 1) == target[...]
    grad[...] = (col[:, 2:3] * (probs - jnp.where(at, 1.0, 0.0))).astype(bf16)
    blocks, per, cols, _ = held.shape
    span = per * cols
    for k in range(blocks):
        send[:, k * span : (k + 1) * span] = block(k).astype(send.dtype)


def keep_kernel(core, grad, words, keep, held, sems):
    block = grad_blocks(core, core[0], grad, words, held, sems)
    blocks, per, cols, _ = held.shape
    span = per * cols
    for k in range(blocks):
        keep[:, k * span : (k + 1) * span] = block(k)


def lift_kernel(core, own, peer, residual, lift, hidden, joined, held, sems):
    blocks, span, _ = held.shape
    half = own.shape[1]
    wait = bring(
        lambda k: lift.at[pl.ds(k * span, span)], lambda k: held.at[k], sems, blocks
    )
    flip = core[0] != 0
    joined[:, :half] = jnp.where(flip, peer[...], own[...])
    joined[:, half:] = jnp.where(flip, own[...], peer[...])
    rows = joined[...].astype(bf16)
    for k in range(blocks):
        wait(k)
        at = slice(k * span, (k + 1) * span)
        hidden[:, at] = (residual[:, at] + over_last(rows, held[k])).astype(bf16)


def lower_kernel(place, parts, hidden, gain, marks, lift, chunks, partial, held, sems):
    blocks, span, _ = held.shape
    wait = bring(
        lambda k: lift.at[pl.ds(k * span, span)], lambda k: held.at[k], sems, blocks
    )
    total = jnp.sum(parts[...].astype(f32), axis=0)
    scale = marks[:, 0:1]
    inner = marks[:, 1:2]
    model = 2 * hidden.shape[1]
    d_res = scale * (total * gain[...])
    d_res = d_res - hidden[...].astype(f32) * (scale * scale * (inner / model))
    high = d_res.astype(bf16)
    low = (d_res - high.astype(f32)).astype(bf16)
    cols = chunks.shape[2] // 2
    for k in range(chunks.shape[0]):
        chunks[k, :, :cols] = high[:, k * cols : (k + 1) * cols]
        chunks[k, :, cols:] = low[:, k * cols : (k + 1) * cols]
    out = jnp.zeros(partial.shape, f32)
    for k in range(blocks):
        wait(k)
        out = out + jnp.dot(
            high[:, k * span : (k + 1) * span], held[k], preferred_element_type=f32
        )
    partial[...] = out


def unit_blocks(weights, mats, held, sems):
    quarters, _, units, _ = weights.shape
    many = len(mats)
    return bring(
        lambda k: weights.at[k // many, mats[k % many]],
        lambda k: held.at[k % many, pl.ds(k // many * units, units)],
        sems,
        quarters * many,
    )


def prepare_kernel(core, latent_t, weights, slope, silu, active, held, sems):
    wait = unit_blocks(weights, (0, 1), held, sems)
    span = weights.shape[2] * 2
    for k in range(2):
        for j in range(4 * k, 4 * k + 4):
            wait(j)
        at = pl.ds(k * span, span)
        gate_pre = jnp.dot(held[0, at], latent_t[...], preferred_element_type=f32)
        up_pre = jnp.dot(held[1, at], latent_t[...], preferred_element_type=f32)
        sig = 1.0 / (1.0 + jnp.exp(-gate_pre))
        silu[at, :] = gate_pre * sig
        slope[at, :] = up_pre * sig * (1.0 + gate_pre * (1.0 - sig))
        active[at, :] = (gate_pre * sig * up_pre).astype(bf16)


def expert_kernel(
    core, own, peer, slope, silu, active, marks_t, weights, keep, send, routed_t, held, sems
):
    half = own.shape[1]
    width, rows = routed_t.shape
    span = weights.shape[2] * 2
    wait = unit_blocks(weights, (2, 0, 1), held, sems)
    gate = jnp.sum(marks_t[...], axis=0, keepdims=True)
    a = (own[...].astype(f32).T * gate).astype(bf16)
    b = (peer[...].astype(f32).T * gate).astype(bf16)

    @pl.when(core[0] == 0)
    def _():
        routed_t[:half, :] = a
        routed_t[half:, :] = b

    @pl.when(core[0] != 0)
    def _():
        routed_t[:half, :] = b
        routed_t[half:, :] = a

    def over_first(x, w):
        return lax.dot_general(x, w, (((0,), (0,)), ((), ())), preferred_element_type=f32)

    term = jnp.zeros((1, rows), f32)
    block = jnp.zeros((rows, width), f32)
    for k in range(2):
        for j in range(6 * k, 6 * k + 6):
            wait(j)
        at = pl.ds(k * span, span)
        act_grad = jnp.dot(held[0, at], routed_t[...], preferred_element_type=f32)
        term = term + jnp.sum(act_grad * active[at, :].astype(f32), axis=0, keepdims=True)
        gate_back = (act_grad * slope[at, :]).astype(bf16)
        up_back = (act_grad * silu[at, :]).astype(bf16)
        block = block + over_first(gate_back, held[1, at]) + over_first(up_back, held[2, at])

    share = term / jnp.where(gate > 0, gate, 1.0)
    gate_grad = jnp.where(marks_t[...] > 0, share, 0.0).T
    keep[:, half:] = gate_grad
    send[:, half:] = gate_grad.astype(bf16)
    flip = core[0] != 0
    keep[:, :half] = jnp.where(flip, block[:, half:], block[:, :half])
    send[:, :half] = jnp.where(flip, block[:, :half], block[:, half:]).astype(bf16)


def mix_kernel(spot, own, peer, keep, other, gates, out):
    groups = gates.shape[0] // 2
    rows = gates.shape[1]
    row = lax.broadcasted_iota(jnp.int32, (128, rows), 0)

    def over_first(x, w):
        return lax.dot_general(x, w, (((0,), (0,)), ((), ())), preferred_element_type=f32)

    for k in range(groups):
        at = slice(k * rows, (k + 1) * rows)
        back = lax.rem(spot[1] + groups - k, groups)
        gate = gates[pl.ds(back, 1), :]
        gate_peer = gates[pl.ds(groups + back, 1), :]
        col = jnp.where(row == 0, gate, gate_peer).T
        part = over_first(own[:, at], keep[...]) * col[:, 0:1]
        out[at, :] = part + over_first(peer[:, at], other[...]) * col[:, 1:2]


def struct(shape, dtype):
    return jax.ShapeDtypeStruct(shape, dtype)


def call(kernel, name, scalar, args, hbm, out_shape, scratch, mib=28, flops=0, choose=None):
    def spec(k, x):
        if k in hbm:
            return pl.BlockSpec(memory_space=pltpu.HBM)
        if choose is not None and k == choose[0]:
            return pl.BlockSpec(*choose[1:])
        return pl.BlockSpec(x.shape, lambda i, core: (0,) * x.ndim)

    def out_spec(x):
        return pl.BlockSpec(x.shape, lambda i, core: (0,) * len(x.shape))

    cost = None
    if flops:
        cost = pl.CostEstimate(flops=flops, bytes_accessed=flops // 512, transcendentals=0)
    args = [
        pltpu.with_memory_space_constraint(x, pltpu.HBM) if k in hbm else x
        for k, x in enumerate(args)
    ]
    return pl.pallas_call(
        kernel,
        grid_spec=pltpu.PrefetchScalarGridSpec(
            num_scalar_prefetch=1,
            grid=(1,),
            in_specs=[spec(k, x) for k, x in enumerate(args)],
            out_specs=[out_spec(x) for x in out_shape],
            scratch_shapes=scratch,
        ),
        out_shape=out_shape,
        compiler_params=pltpu.CompilerParams(vmem_limit_bytes=mib << 20),
        cost_estimate=cost,
        name=name,
    )(scalar, *args)


def block_scratch(blocks, shape):
    return [pltpu.VMEM((blocks,) + shape, bf16), pltpu.SemaphoreType.DMA((blocks,))]


def call_head(core, own, peer, gain, words, target):
    rows = own.shape[0]
    places, _, cols, count = words.shape
    blocks = gain.shape[0]
    return call(
        head_kernel,
        "head",
        core,
        (own, peer, gain, words, target),
        (3,),
        [struct((rows, count), f32), struct((8, 128), f32), struct((rows, 128), f32)],
        block_scratch(blocks, (2 * places // blocks, cols, count)),
    )


def call_loss(core, stats, logits, target, cot, scale, words):
    places, _, cols, count = words.shape
    rows = logits.shape[0]
    return call(
        loss_kernel,
        "loss",
        core,
        (stats, logits, target, cot, scale, words),
        (5,),
        [
            struct((rows, count), bf16),
            struct((rows, places * cols), bf16),
            struct((8, rows), f32),
            struct((rows, 128), f32),
        ],
        block_scratch(4, (places // 4, cols, count)),
    )


def call_keep(core, grad, words):
    places, _, cols, count = words.shape
    rows = grad.shape[0]
    return call(
        keep_kernel,
        "keep",
        core,
        (grad, words),
        (1,),
        [struct((rows, places * cols), f32)],
        block_scratch(4, (places // 4, cols, count)),
        flops=places * cols * rows * count * 2,
    )[0]


def call_lift(core, own, peer, residual, lift):
    wide, width = lift.shape
    return call(
        lift_kernel,
        "lift",
        core,
        (own.astype(f32), peer.astype(f32), residual, lift),
        (3,),
        [struct(residual.shape, bf16)],
        [pltpu.VMEM((own.shape[0], width), f32)] + block_scratch(4, (wide // 4, width)),
    )[0]


def call_lower(place, parts, hidden, gain, marks, lift):
    places, chunk, wide = parts.shape
    width = lift.shape[1]
    return call(
        lower_kernel,
        "lower",
        place,
        (parts, hidden, gain, marks, lift),
        (4,),
        [struct((places, chunk, 2 * (wide // places)), bf16), struct((chunk, width), f32)],
        block_scratch(4, (wide // 4, width)),
        choose=(3, (chunk, 128), lambda i, place: (place[0], 0)),
    )


def unit_scratch(weights, mats):
    quarters, _, units, width = weights.shape
    return [
        pltpu.VMEM((mats, quarters * units, width), bf16),
        pltpu.SemaphoreType.DMA((quarters * mats,)),
    ]


def call_prepare(core, latent_t, weights):
    width, rows = latent_t.shape
    quarters, _, units, _ = weights.shape
    shape = (quarters * units, rows)
    return call(
        prepare_kernel,
        "prepare",
        core,
        (latent_t, weights),
        (1,),
        [struct(shape, f32), struct(shape, f32), struct(shape, bf16)],
        unit_scratch(weights, 2),
        flops=4 * rows * width * quarters * units,
    )


def call_expert(core, own, peer, prepared, marks_t, weights):
    rows, half = own.shape
    lanes = half + marks_t.shape[0]
    return call(
        expert_kernel,
        "expert",
        core,
        (own, peer) + tuple(prepared) + (marks_t, weights),
        (6,),
        [struct((rows, lanes), f32), struct((rows, lanes), bf16)],
        [pltpu.VMEM((2 * half, rows), bf16)] + unit_scratch(weights, 3),
    )


def call_mix(core, own, peer, keep, other, gates):
    shape = (own.shape[1], keep.shape[1])
    return call(
        mix_kernel, "mix", core, (own, peer, keep, other, gates), (), [struct(shape, f32)], []
    )[0]


def on_device(
    latent,
    residual,
    gates,
    route_ids,
    w_gate,
    w_up,
    w_out,
    w_lift,
    norm_gain,
    w_vocab,
    targets,
    loss_cot,
):
    core = lax.axis_index("c")
    own_index = lax.axis_index(slab)
    place = lax.axis_index(plane)
    places = lax.axis_size(plane)
    groups = lax.axis_size("dp")
    rows, width = latent.shape
    half = width // 2
    cols = residual.shape[1]
    words = w_vocab.shape[1]
    chunk = rows // places
    wide = places * cols
    first = core == 0

    def mine(x, axis):
        a, b = jnp.split(x, 2, axis)
        return jnp.where(first, a, b)

    def other(x, axis):
        a, b = jnp.split(x, 2, axis)
        return jnp.where(first, b, a)

    def joined(own, peer, axis):
        return jnp.where(
            first,
            jnp.concatenate([own, peer], axis),
            jnp.concatenate([peer, own], axis),
        )

    gate_mat, up_mat, out_mat = w_gate[0], w_up[0], w_out[0]
    lift_t = w_lift.T
    ring = lax.axis_size("y")
    around = [lift_t] + [
        lax.ppermute(lift_t, "y", [((i + k) % ring, i) for i in range(ring)])
        for k in range(1, ring)
    ]

    gate_marks = jnp.where(route_ids.T == own_index, gates.T, 0.0)
    gate_own = jnp.sum(gate_marks, axis=0)
    ahead = [gate_own] + [
        lax.ppermute(gate_own, "dp", [(i, (i + k) % groups) for i in range(groups)])
        for k in range(1, groups)
    ]
    out_keep = mine(out_mat, 1)
    out_peer = swap(other(out_mat, 1))

    lat_own = spread(mine(latent, 1), "dp")
    *ahead, lat_own = lax.optimization_barrier((*ahead, lat_own))
    lat_peer = swap(lat_own)
    turn = (ring - lax.axis_index("y")) % ring
    *around, lat_own = lax.optimization_barrier((*around, lat_own))
    lift_deep = lax.dynamic_slice_in_dim(jnp.stack(around + around), turn, ring, 0)
    lift_wide = lax.all_gather(lift_deep, "z", axis=0, tiled=True).reshape(wide, width)

    lat_all = joined(lat_own, lat_peer, 2).reshape(-1, width)
    gate_part = dot(lat_all, gate_mat, 1, 0)
    up_part = dot(lat_all, up_mat, 1, 0)
    active = (jax.nn.silu(gate_part) * up_part).astype(bf16)
    core_id = core.astype(jnp.int32)[None]
    ahead = jnp.stack(ahead)
    gate_rows = jnp.concatenate([ahead, swap(ahead)])
    spot = jnp.stack([core, lax.axis_index("dp")]).astype(jnp.int32)
    active_t = active.T
    part = call_mix(spot, active_t, swap(active_t), out_keep, out_peer, gate_rows)
    part, gate_mat, up_mat, out_mat = lax.optimization_barrier((part, gate_mat, up_mat, out_mat))
    weights = jnp.stack([gate_mat.T, up_mat.T, out_mat])
    summed = jnp.sum(deal(part, "dp").reshape(groups, rows, half), axis=0)

    summed, weights = lax.optimization_barrier((summed, weights))
    weights = lax.all_gather(weights, "dp")

    summed = summed.reshape(places, chunk, half)
    carried = residual.reshape(places, chunk, cols).astype(f32)
    carried = jnp.pad(carried, ((0, 0), (0, 0), (0, 128 - cols)))
    dealt = deal(jnp.concatenate([summed, carried], axis=2), plane)
    comb_own = jnp.sum(dealt[:, :, :half], axis=0).astype(bf16)
    res_rows = dealt[:, :, half : half + cols].transpose(1, 0, 2).reshape(chunk, wide)
    hidden = call_lift(core_id, comb_own, swap(comb_own), res_rows, lift_wide)
    hid_own = spread(spread(hidden, "z"), "y").transpose(1, 0, 2, 3).reshape(rows, wide)

    steps = 2
    gain_sides = norm_gain.astype(f32).reshape(places, 2, cols)
    gain_own = jnp.where(first, gain_sides[:, 0], gain_sides[:, 1]).reshape(steps, -1)
    gain_peer = jnp.where(first, gain_sides[:, 1], gain_sides[:, 0]).reshape(steps, -1)
    target = (targets - own_index * words)[:, None]
    vocab = w_vocab.reshape(places, 2, cols, words)
    logits, stats, scale = call_head(
        core_id, hid_own, swap(hid_own), jnp.concatenate([gain_own, gain_peer]), vocab, target
    )
    stats_all = spread(stats, slab)
    grad, send, loss, marks = call_loss(
        core_id, stats_all, logits, target, loss_cot[None], scale, vocab
    )
    row_loss = loss[0]
    keep = call_keep(core_id, grad, vocab)
    keep = (keep + swap(send).astype(f32)).astype(bf16)
    parts = deal(keep.reshape(places, chunk, wide), plane)
    prepared = call_prepare(core_id, latent.T, weights)
    parts, *prepared = lax.optimization_barrier((parts, *prepared))
    chunks, partial = call_lower(
        place.astype(jnp.int32)[None], parts, hidden, gain_own.reshape(1, wide), marks, lift_wide
    )
    cg_rows = (mine(partial, 1) + swap(other(partial, 1))).astype(bf16)
    cg_rows = jnp.broadcast_to(cg_rows[None], (places, chunk, half))
    dealt = deal(jnp.concatenate([cg_rows, chunks], axis=2), plane)
    cg_own = dealt[:, :, :half].reshape(rows, half)
    d_residual = dealt[:, :, half : half + cols].astype(f32) + dealt[:, :, half + cols :].astype(f32)
    d_residual = d_residual.reshape(rows, cols)

    gate_marks = jnp.pad(gate_marks, ((0, 128 - gate_marks.shape[0]), (0, 0)))
    keep, send = call_expert(core_id, cg_own, swap(cg_own), prepared, gate_marks, weights)
    keep = (keep + swap(send).astype(f32)).astype(bf16)
    tail = jnp.sum(deal(keep, plane).astype(f32).reshape(places, chunk, -1), axis=0).astype(bf16)
    tail = spread(tail, plane).reshape(rows, -1)
    d_latent = joined(tail[:, :half], swap(tail[:, :half]), 1).astype(f32)
    d_gates = tail[:, half : half + gates.shape[1]].astype(f32)
    return (row_loss, d_residual, d_latent, d_gates)


def solution(mesh):
    fine = Mesh(mesh.devices.reshape(mesh.devices.shape[0], 8, 4, 2), ("dp", "z", "y", "c"))
    in_specs = (
        P("dp", None),
        P("dp", slab),
        P("dp", None),
        P("dp", None),
        P(slab, None, "dp"),
        P(slab, None, "dp"),
        P(slab, "dp", None),
        P(None, slab),
        P(),
        P(None, slab),
        P("dp"),
        P("dp"),
    )
    out_specs = (P("dp"), P("dp", slab), P("dp", None), P("dp", None))
    return jax.shard_map(
        on_device, mesh=fine, in_specs=in_specs, out_specs=out_specs, check_vma=False
    )
```

```python
import jax
import jax.numpy as jnp
from jax import lax
from jax.experimental import pallas as pl
from jax.experimental.pallas import tpu as pltpu
from jax.sharding import Mesh, PartitionSpec as P

norm_epsilon = 1e-05
plane = ("z", "y")
slab = ("z", "y", "c")
bf16 = jnp.bfloat16
f32 = jnp.float32


def dot(a, b, ca, cb):
    return lax.dot_general(a, b, (((ca,), (cb,)), ((), ())), preferred_element_type=f32)


def swap(x):
    return lax.ppermute(x, "c", [(0, 1), (1, 0)])


def deal(x, axes):
    return lax.all_to_all(x, axes, 0, 0, tiled=True)


def spread(x, axes):
    count = lax.axis_size(axes)
    return deal(jnp.broadcast_to(x[None], (count,) + x.shape), axes)


def over_last(x, w):
    return lax.dot_general(x, w, (((1,), (1,)), ((), ())), preferred_element_type=f32)


def bring(source, buffers, sems, count):
    copies = [pltpu.make_async_copy(source(k), buffers(k), sems.at[k]) for k in range(count)]
    for copy in copies:
        copy.start()
    return lambda k: copies[k].wait()


def head_kernel(core, own, peer, gain, words, target, logits, stats, scale, held, sems):
    rows, wide = own.shape
    blocks, per, cols, count = held.shape
    span = per * cols
    half = wide // span

    def source(k):
        side = core[0] if k < half else 1 - core[0]
        return words.at[pl.ds(k % half * per, per), side]

    wait = bring(source, lambda k: held.at[k], sems, blocks)
    total = jnp.zeros((rows, 128), f32)
    for k in range(wide // 128):
        a = own[:, k * 128 : (k + 1) * 128].astype(f32)
        b = peer[:, k * 128 : (k + 1) * 128].astype(f32)
        total = total + a * a + b * b
    mean = jnp.sum(total, axis=1, keepdims=True) / (2 * wide) + norm_epsilon
    guess = lax.rsqrt(mean)
    guess = guess * (1.5 - 0.5 * mean * guess * guess)
    scale[...] = jnp.broadcast_to(guess, scale.shape)
    for k in range(blocks):
        side = own if k < half else peer
        at = k % half * span
        h = side[:, at : at + span].astype(f32)
        h = (h * guess * gain[k : k + 1]).astype(bf16)
        wait(k)
        part = jnp.dot(h, held[k].reshape(span, count), preferred_element_type=f32)
        logits[...] = part if k == 0 else logits[...] + part

    values = logits[...]
    peak = jnp.max(values, axis=1, keepdims=True)
    below = values - peak
    weight = jnp.exp(below)
    total = jnp.sum(weight, axis=1, keepdims=True)
    lean = jnp.sum(weight * below, axis=1, keepdims=True)
    at = lax.broadcasted_iota(jnp.int32, values.shape, 1) == target[...]
    hit = jnp.sum(jnp.where(at, values, 0.0), axis=1, keepdims=True)
    lane = lax.broadcasted_iota(jnp.int32, (rows, 128), 1)
    packed = jnp.where(lane == 0, peak, jnp.where(lane == 1, total, 0.0))
    packed = jnp.where(lane == 2, lean, jnp.where(lane == 3, hit, packed))
    packed = packed.T
    stats[0:4, :] = packed[0:4, 0:128]
    stats[4:8, :] = packed[0:4, 128:256]


def grad_blocks(core, side, grad, words, held, sems):
    blocks, per, cols, count = held.shape
    wait = bring(
        lambda k: words.at[pl.ds(k * per, per), side], lambda k: held.at[k], sems, blocks
    )

    def block(k):
        wait(k)
        return over_last(grad[...], held[k].reshape(per * cols, count))

    return block


def loss_kernel(
    core, stats, logits, target, cot, scale, words, grad, send, loss, marks, held, sems
):
    block = grad_blocks(core, 1 - core[0], grad, words, held, sems)

    def stat(k):
        return jnp.concatenate([stats[:, k, :], stats[:, k + 4, :]], axis=1)

    peaks = stat(0)
    peak = jnp.max(peaks, axis=0, keepdims=True)
    gap = peaks - peak
    share = jnp.exp(gap)
    totals = stat(1)
    total = jnp.sum(share * totals, axis=0, keepdims=True)
    lean = jnp.sum(share * (stat(2) + gap * totals), axis=0, keepdims=True)
    hit = jnp.sum(stat(3), axis=0, keepdims=True)
    inverse = 1.0 / total
    inner = cot[...] * (lean * inverse - (hit - peak))
    row = lax.broadcasted_iota(jnp.int32, (128, peak.shape[1]), 0)
    packed = jnp.where(row == 0, peak, jnp.where(row == 1, inverse, 0.0))
    packed = jnp.where(row == 2, cot[...], jnp.where(row == 3, inner, packed))
    col = packed.T
    loss[...] = jnp.broadcast_to(peak + jnp.log(total) - hit, loss.shape)
    lane = lax.broadcasted_iota(jnp.int32, marks.shape, 1)
    marks[...] = jnp.where(lane == 0, scale[...], col[:, 3:4])
    probs = jnp.exp(logits[...] - col[:, 0:1]) * col[:, 1:2]
    at = lax.broadcasted_iota(jnp.int32, probs.shape, 1) == target[...]
    grad[...] = (col[:, 2:3] * (probs - jnp.where(at, 1.0, 0.0))).astype(bf16)
    blocks, per, cols, _ = held.shape
    span = per * cols
    for k in range(blocks):
        send[:, k * span : (k + 1) * span] = block(k).astype(send.dtype)


def keep_kernel(core, grad, words, keep, held, sems):
    block = grad_blocks(core, core[0], grad, words, held, sems)
    blocks, per, cols, _ = held.shape
    span = per * cols
    for k in range(blocks):
        keep[:, k * span : (k + 1) * span] = block(k)


def lift_kernel(core, own, peer, residual, lift, hidden, joined, held, sems):
    blocks, span, _ = held.shape
    half = own.shape[1]
    wait = bring(
        lambda k: lift.at[pl.ds(k * span, span)], lambda k: held.at[k], sems, blocks
    )
    flip = core[0] != 0
    joined[:, :half] = jnp.where(flip, peer[...], own[...])
    joined[:, half:] = jnp.where(flip, own[...], peer[...])
    rows = joined[...].astype(bf16)
    for k in range(blocks):
        wait(k)
        at = slice(k * span, (k + 1) * span)
        hidden[:, at] = (residual[:, at] + over_last(rows, held[k])).astype(bf16)


def lower_kernel(place, parts, hidden, gain, marks, lift, chunks, partial, held, sems):
    blocks, span, _ = held.shape
    wait = bring(
        lambda k: lift.at[pl.ds(k * span, span)], lambda k: held.at[k], sems, blocks
    )
    total = jnp.sum(parts[...].astype(f32), axis=0)
    scale = marks[:, 0:1]
    inner = marks[:, 1:2]
    model = 2 * hidden.shape[1]
    d_res = scale * (total * gain[...])
    d_res = d_res - hidden[...].astype(f32) * (scale * scale * (inner / model))
    high = d_res.astype(bf16)
    low = (d_res - high.astype(f32)).astype(bf16)
    cols = chunks.shape[2] // 2
    for k in range(chunks.shape[0]):
        chunks[k, :, :cols] = high[:, k * cols : (k + 1) * cols]
        chunks[k, :, cols:] = low[:, k * cols : (k + 1) * cols]
    out = jnp.zeros(partial.shape, f32)
    for k in range(blocks):
        wait(k)
        out = out + jnp.dot(
            high[:, k * span : (k + 1) * span], held[k], preferred_element_type=f32
        )
    partial[...] = out


def unit_blocks(weights, mats, held, sems):
    quarters, _, units, _ = weights.shape
    many = len(mats)
    return bring(
        lambda k: weights.at[k // many, mats[k % many]],
        lambda k: held.at[k % many, pl.ds(k // many * units, units)],
        sems,
        quarters * many,
    )


def prepare_kernel(core, latent_t, weights, slope, silu, active, held, sems):
    wait = unit_blocks(weights, (0, 1), held, sems)
    span = weights.shape[2] * 2
    for k in range(2):
        for j in range(4 * k, 4 * k + 4):
            wait(j)
        at = pl.ds(k * span, span)
        gate_pre = jnp.dot(held[0, at], latent_t[...], preferred_element_type=f32)
        up_pre = jnp.dot(held[1, at], latent_t[...], preferred_element_type=f32)
        sig = 1.0 / (1.0 + jnp.exp(-gate_pre))
        silu[at, :] = gate_pre * sig
        slope[at, :] = up_pre * sig * (1.0 + gate_pre * (1.0 - sig))
        active[at, :] = (gate_pre * sig * up_pre).astype(bf16)


def expert_kernel(
    core, own, peer, slope, silu, active, marks_t, weights, keep, send, routed_t, held, sems
):
    half = own.shape[1]
    width, rows = routed_t.shape
    span = weights.shape[2] * 2
    wait = unit_blocks(weights, (2, 0, 1), held, sems)
    gate = jnp.sum(marks_t[...], axis=0, keepdims=True)
    a = (own[...].astype(f32).T * gate).astype(bf16)
    b = (peer[...].astype(f32).T * gate).astype(bf16)

    @pl.when(core[0] == 0)
    def _():
        routed_t[:half, :] = a
        routed_t[half:, :] = b

    @pl.when(core[0] != 0)
    def _():
        routed_t[:half, :] = b
        routed_t[half:, :] = a

    def over_first(x, w):
        return lax.dot_general(x, w, (((0,), (0,)), ((), ())), preferred_element_type=f32)

    term = jnp.zeros((1, rows), f32)
    block = jnp.zeros((rows, width), f32)
    for k in range(2):
        for j in range(6 * k, 6 * k + 6):
            wait(j)
        at = pl.ds(k * span, span)
        act_grad = jnp.dot(held[0, at], routed_t[...], preferred_element_type=f32)
        term = term + jnp.sum(act_grad * active[at, :].astype(f32), axis=0, keepdims=True)
        gate_back = (act_grad * slope[at, :]).astype(bf16)
        up_back = (act_grad * silu[at, :]).astype(bf16)
        block = block + over_first(gate_back, held[1, at]) + over_first(up_back, held[2, at])

    share = term / jnp.where(gate > 0, gate, 1.0)
    gate_grad = jnp.where(marks_t[...] > 0, share, 0.0).T
    keep[:, half:] = gate_grad
    send[:, half:] = gate_grad.astype(bf16)
    flip = core[0] != 0
    keep[:, :half] = jnp.where(flip, block[:, half:], block[:, :half])
    send[:, :half] = jnp.where(flip, block[:, :half], block[:, half:]).astype(bf16)


def mix_kernel(spot, own, peer, keep, other, gates, out):
    groups = gates.shape[0] // 2
    rows = gates.shape[1]
    row = lax.broadcasted_iota(jnp.int32, (128, rows), 0)

    def over_first(x, w):
        return lax.dot_general(x, w, (((0,), (0,)), ((), ())), preferred_element_type=f32)

    for k in range(groups):
        at = slice(k * rows, (k + 1) * rows)
        back = lax.rem(spot[1] + groups - k, groups)
        gate = gates[pl.ds(back, 1), :]
        gate_peer = gates[pl.ds(groups + back, 1), :]
        col = jnp.where(row == 0, gate, gate_peer).T
        part = over_first(own[:, at], keep[...]) * col[:, 0:1]
        out[at, :] = part + over_first(peer[:, at], other[...]) * col[:, 1:2]


def struct(shape, dtype):
    return jax.ShapeDtypeStruct(shape, dtype)


def call(kernel, name, scalar, args, hbm, out_shape, scratch, mib=28, flops=0, choose=None):
    def spec(k, x):
        if k in hbm:
            return pl.BlockSpec(memory_space=pltpu.HBM)
        if choose is not None and k == choose[0]:
            return pl.BlockSpec(*choose[1:])
        return pl.BlockSpec(x.shape, lambda i, core: (0,) * x.ndim)

    def out_spec(x):
        return pl.BlockSpec(x.shape, lambda i, core: (0,) * len(x.shape))

    cost = None
    if flops:
        cost = pl.CostEstimate(flops=flops, bytes_accessed=flops // 512, transcendentals=0)
    args = [
        pltpu.with_memory_space_constraint(x, pltpu.HBM) if k in hbm else x
        for k, x in enumerate(args)
    ]
    return pl.pallas_call(
        kernel,
        grid_spec=pltpu.PrefetchScalarGridSpec(
            num_scalar_prefetch=1,
            grid=(1,),
            in_specs=[spec(k, x) for k, x in enumerate(args)],
            out_specs=[out_spec(x) for x in out_shape],
            scratch_shapes=scratch,
        ),
        out_shape=out_shape,
        compiler_params=pltpu.CompilerParams(vmem_limit_bytes=mib << 20),
        cost_estimate=cost,
        name=name,
    )(scalar, *args)


def block_scratch(blocks, shape):
    return [pltpu.VMEM((blocks,) + shape, bf16), pltpu.SemaphoreType.DMA((blocks,))]


def call_head(core, own, peer, gain, words, target):
    rows = own.shape[0]
    places, _, cols, count = words.shape
    blocks = gain.shape[0]
    return call(
        head_kernel,
        "head",
        core,
        (own, peer, gain, words, target),
        (3,),
        [struct((rows, count), f32), struct((8, 128), f32), struct((rows, 128), f32)],
        block_scratch(blocks, (2 * places // blocks, cols, count)),
    )


def call_loss(core, stats, logits, target, cot, scale, words):
    places, _, cols, count = words.shape
    rows = logits.shape[0]
    return call(
        loss_kernel,
        "loss",
        core,
        (stats, logits, target, cot, scale, words),
        (5,),
        [
            struct((rows, count), bf16),
            struct((rows, places * cols), bf16),
            struct((8, rows), f32),
            struct((rows, 128), f32),
        ],
        block_scratch(4, (places // 4, cols, count)),
    )


def call_keep(core, grad, words):
    places, _, cols, count = words.shape
    rows = grad.shape[0]
    return call(
        keep_kernel,
        "keep",
        core,
        (grad, words),
        (1,),
        [struct((rows, places * cols), f32)],
        block_scratch(4, (places // 4, cols, count)),
        flops=places * cols * rows * count * 2,
    )[0]


def call_lift(core, own, peer, residual, lift):
    wide, width = lift.shape
    return call(
        lift_kernel,
        "lift",
        core,
        (own.astype(f32), peer.astype(f32), residual, lift),
        (3,),
        [struct(residual.shape, bf16)],
        [pltpu.VMEM((own.shape[0], width), f32)] + block_scratch(4, (wide // 4, width)),
    )[0]


def call_lower(place, parts, hidden, gain, marks, lift, places):
    _, chunk, wide = parts.shape
    width = lift.shape[1]
    return call(
        lower_kernel,
        "lower",
        place,
        (parts, hidden, gain, marks, lift),
        (4,),
        [struct((places, chunk, 2 * (wide // places)), bf16), struct((chunk, width), f32)],
        block_scratch(4, (wide // 4, width)),
        choose=(3, (chunk, 128), lambda i, place: (place[0], 0)),
    )


def unit_scratch(weights, mats):
    quarters, _, units, width = weights.shape
    return [
        pltpu.VMEM((mats, quarters * units, width), bf16),
        pltpu.SemaphoreType.DMA((quarters * mats,)),
    ]


def call_prepare(core, latent_t, weights):
    width, rows = latent_t.shape
    quarters, _, units, _ = weights.shape
    shape = (quarters * units, rows)
    return call(
        prepare_kernel,
        "prepare",
        core,
        (latent_t, weights),
        (1,),
        [struct(shape, f32), struct(shape, f32), struct(shape, bf16)],
        unit_scratch(weights, 2),
        flops=4 * rows * width * quarters * units,
    )


def call_expert(core, own, peer, prepared, marks_t, weights):
    rows, half = own.shape
    lanes = half + marks_t.shape[0]
    return call(
        expert_kernel,
        "expert",
        core,
        (own, peer) + tuple(prepared) + (marks_t, weights),
        (6,),
        [struct((rows, lanes), f32), struct((rows, lanes), bf16)],
        [pltpu.VMEM((2 * half, rows), bf16)] + unit_scratch(weights, 3),
    )


def call_mix(core, own, peer, keep, other, gates):
    shape = (own.shape[1], keep.shape[1])
    return call(
        mix_kernel, "mix", core, (own, peer, keep, other, gates), (), [struct(shape, f32)], []
    )[0]


def on_device(
    latent,
    residual,
    gates,
    route_ids,
    w_gate,
    w_up,
    w_out,
    w_lift,
    norm_gain,
    w_vocab,
    targets,
    loss_cot,
):
    core = lax.axis_index("c")
    own_index = lax.axis_index(slab)
    place = lax.axis_index(plane)
    places = lax.axis_size(plane)
    groups = lax.axis_size("dp")
    rows, width = latent.shape
    half = width // 2
    cols = residual.shape[1]
    words = w_vocab.shape[1]
    chunk = rows // places
    wide = places * cols
    first = core == 0

    def mine(x, axis):
        a, b = jnp.split(x, 2, axis)
        return jnp.where(first, a, b)

    def other(x, axis):
        a, b = jnp.split(x, 2, axis)
        return jnp.where(first, b, a)

    def joined(own, peer, axis):
        return jnp.where(
            first,
            jnp.concatenate([own, peer], axis),
            jnp.concatenate([peer, own], axis),
        )

    gate_mat, up_mat, out_mat = w_gate[0], w_up[0], w_out[0]
    lift_t = w_lift.T
    ring = lax.axis_size("y")
    around = [lift_t] + [
        lax.ppermute(lift_t, "y", [((i + k) % ring, i) for i in range(ring)])
        for k in range(1, ring)
    ]

    gate_marks = jnp.where(route_ids.T == own_index, gates.T, 0.0)
    gate_own = jnp.sum(gate_marks, axis=0)
    ahead = [gate_own] + [
        lax.ppermute(gate_own, "dp", [(i, (i + k) % groups) for i in range(groups)])
        for k in range(1, groups)
    ]
    out_keep = mine(out_mat, 1)
    out_peer = swap(other(out_mat, 1))

    lat_own = spread(mine(latent, 1), "dp")
    *ahead, lat_own = lax.optimization_barrier((*ahead, lat_own))
    lat_peer = swap(lat_own)
    turn = (ring - lax.axis_index("y")) % ring
    *around, lat_own = lax.optimization_barrier((*around, lat_own))
    lift_deep = lax.dynamic_slice_in_dim(jnp.stack(around + around), turn, ring, 0)
    lift_wide = lax.all_gather(lift_deep, "z", axis=0, tiled=True).reshape(wide, width)

    lat_all = joined(lat_own, lat_peer, 2).reshape(-1, width)
    gate_part = dot(lat_all, gate_mat, 1, 0)
    up_part = dot(lat_all, up_mat, 1, 0)
    active = (jax.nn.silu(gate_part) * up_part).astype(bf16)
    core_id = core.astype(jnp.int32)[None]
    ahead = jnp.stack(ahead)
    gate_rows = jnp.concatenate([ahead, swap(ahead)])
    spot = jnp.stack([core, lax.axis_index("dp")]).astype(jnp.int32)
    active_t = active.T
    part = call_mix(spot, active_t, swap(active_t), out_keep, out_peer, gate_rows)
    part, gate_mat, up_mat, out_mat = lax.optimization_barrier((part, gate_mat, up_mat, out_mat))
    weights = jnp.stack([gate_mat.T, up_mat.T, out_mat])
    summed = jnp.sum(deal(part, "dp").reshape(groups, rows, half), axis=0)

    summed, weights = lax.optimization_barrier((summed, weights))
    weights = lax.all_gather(weights, "dp")

    summed = summed.reshape(places, chunk, half)
    carried = residual.reshape(places, chunk, cols).astype(f32)
    carried = jnp.pad(carried, ((0, 0), (0, 0), (0, 128 - cols)))
    dealt = deal(jnp.concatenate([summed, carried], axis=2), plane)
    comb_own = jnp.sum(dealt[:, :, :half], axis=0).astype(bf16)
    res_rows = dealt[:, :, half : half + cols].transpose(1, 0, 2).reshape(chunk, wide)
    hidden = call_lift(core_id, comb_own, swap(comb_own), res_rows, lift_wide)
    hid_own = spread(spread(hidden, "z"), "y").transpose(1, 0, 2, 3).reshape(rows, wide)

    steps = 2
    gain_sides = norm_gain.astype(f32).reshape(places, 2, cols)
    gain_own = jnp.where(first, gain_sides[:, 0], gain_sides[:, 1]).reshape(steps, -1)
    gain_peer = jnp.where(first, gain_sides[:, 1], gain_sides[:, 0]).reshape(steps, -1)
    target = (targets - own_index * words)[:, None]
    vocab = w_vocab.reshape(places, 2, cols, words)
    logits, stats, scale = call_head(
        core_id, hid_own, swap(hid_own), jnp.concatenate([gain_own, gain_peer]), vocab, target
    )
    stats_all = spread(stats, slab)
    grad, send, loss, marks = call_loss(
        core_id, stats_all, logits, target, loss_cot[None], scale, vocab
    )
    row_loss = loss[0]
    keep = call_keep(core_id, grad, vocab)
    keep = (keep + swap(send).astype(f32)).astype(bf16)
    keep = keep.reshape(places // ring, ring, chunk, wide).transpose(1, 0, 2, 3)
    keep = jnp.sum(deal(keep, "y").astype(f32), axis=0).astype(bf16)
    parts = deal(keep, "z")
    prepared = call_prepare(core_id, latent.T, weights)
    parts, *prepared = lax.optimization_barrier((parts, *prepared))
    chunks, partial = call_lower(
        place.astype(jnp.int32)[None], parts, hidden, gain_own.reshape(1, wide), marks, lift_wide, places
    )
    cg_rows = (mine(partial, 1) + swap(other(partial, 1))).astype(bf16)
    cg_rows = jnp.broadcast_to(cg_rows[None], (places, chunk, half))
    dealt = deal(jnp.concatenate([cg_rows, chunks], axis=2), plane)
    cg_own = dealt[:, :, :half].reshape(rows, half)
    d_residual = dealt[:, :, half : half + cols].astype(f32) + dealt[:, :, half + cols :].astype(f32)
    d_residual = d_residual.reshape(rows, cols)

    gate_marks = jnp.pad(gate_marks, ((0, 128 - gate_marks.shape[0]), (0, 0)))
    keep, send = call_expert(core_id, cg_own, swap(cg_own), prepared, gate_marks, weights)
    keep = (keep + swap(send).astype(f32)).astype(bf16)
    tail = jnp.sum(deal(keep, plane).astype(f32).reshape(places, chunk, -1), axis=0).astype(bf16)
    tail = spread(tail, plane).reshape(rows, -1)
    d_latent = joined(tail[:, :half], swap(tail[:, :half]), 1).astype(f32)
    d_gates = tail[:, half : half + gates.shape[1]].astype(f32)
    return (row_loss, d_residual, d_latent, d_gates)


def solution(mesh):
    fine = Mesh(mesh.devices.reshape(mesh.devices.shape[0], 8, 4, 2), ("dp", "z", "y", "c"))
    in_specs = (
        P("dp", None),
        P("dp", slab),
        P("dp", None),
        P("dp", None),
        P(slab, None, "dp"),
        P(slab, None, "dp"),
        P(slab, "dp", None),
        P(None, slab),
        P(),
        P(None, slab),
        P("dp"),
        P("dp"),
    )
    out_specs = (P("dp"), P("dp", slab), P("dp", None), P("dp", None))
    return jax.shard_map(
        on_device, mesh=fine, in_specs=in_specs, out_specs=out_specs, check_vma=False
    )
```
